32 devices in a mesh: mp: 4 (over z), dp: 8 (over y, x, core).
Axes of the slice: x: 2, y: 2, z: 4, core: 2. Of those that a mesh axis runs over, the one named last changes fastest.
Arguments:
- volume: bfloat16 [8, 64, 64, 2048], P('dp', 'mp'), may hold values from -6 to 6
- kernel_a: bfloat16 [3, 3, 3, 32, 64], replicated, may hold values from -0.21875 to 0.21875
- kernel_b: bfloat16 [3, 3, 3, 64, 128], P(None, None, None, 'mp'), may hold values from -0.15625 to 0.15625
- cotangent: bfloat16 [8, 16, 16, 16, 128], P('dp', None, None, None, 'mp'), may hold values from -6 to 6
Outputs:
- features: bfloat16 [8, 16, 16, 16, 128], P('dp', None, None, None, 'mp')
- grad_a: float32 [3, 3, 3, 32, 64], replicated
- grad_b: float32 [3, 3, 3, 64, 128], P(None, None, None, 'mp')
The draws below stay inside these ranges and needn't reach their ends.
All inputs are finite; a program needn't handle non-finite values.
Results may differ from the reference program's by a relative error of at most 0.0049.
Values may be sent and summed in bfloat16 or wider, within the bound.
No kernel may reach another device: no remote copies, remote signals or barrier semaphores. Data moves between devices by JAX's collectives and lax.ppermute only.
A program may use at most 192 MiB of HBM per device.

```python
import math
import jax
import jax.numpy as jnp
from jax import lax

C0 = 32
C1 = 64
C2 = 128
GRID = 64
SAMPLES = 8


def block_levels(key, extent, cuts, least, high):
    factor_of = 1.0
    for position, parts in cuts:
        steps = jax.random.uniform(jax.random.fold_in(jax.random.fold_in(key, 6), position), (parts,), jnp.float32, least / len(cuts), high / len(cuts))
        factor_of = factor_of * jnp.repeat(jnp.exp(steps), extent[position] // parts).reshape((-1,) + (1,) * (len(extent) - 1 - position))
    return factor_of


def gaussian(stream_key, dims, spread, bound, pieces=(), dtype=jnp.bfloat16):
    entries = jax.random.normal(stream_key, dims, jnp.float32) * spread
    if len(pieces) > 0:
        entries = block_levels(stream_key, dims, pieces, -0.22, 0.18) * entries
    return jnp.clip(entries, min=-bound, max=bound).astype(dtype)


def setup_inputs(seed: int = 0) -> dict:
    seeds = jax.random.split(jax.random.key(seed), 5)
    volume = gaussian(seeds[0], (SAMPLES, GRID, GRID, GRID * C0), 1.0, 6.0, ((0, 8), (1, 4)))
    kernel_a = gaussian(seeds[1], (3, 3, 3, C0, C1), (27 * C0) ** -0.5, 0.21875)
    kernel_b = gaussian(seeds[2], (3, 3, 3, C1, C2), (27 * C1) ** -0.5, 0.15625, ((3, 4),))
    cotangent = gaussian(seeds[3], (SAMPLES, GRID // 4, GRID // 4, GRID // 4, C2), 1.0, 6.0, ((0, 8), (4, 4)))
    return dict(volume=volume, kernel_a=kernel_a, kernel_b=kernel_b, cotangent=cotangent)


def forward_conv(padded, kernel):
    return lax.conv_general_dilated(padded, kernel, (2, 2, 2), 'VALID', dimension_numbers=('NDHWC', 'DHWIO', 'NDHWC'), precision=lax.Precision.HIGHEST, preferred_element_type=jnp.float32)

def kernel_grad(padded, grads):
    result = lax.conv_general_dilated(padded, grads, (1, 1, 1), 'VALID', rhs_dilation=(2, 2, 2), dimension_numbers=('CDHWN', 'IDHWO', 'NDHWC'), precision=lax.Precision.HIGHEST, preferred_element_type=jnp.float32)
    return jnp.transpose(result, (1, 2, 3, 0, 4))

def input_grad(grads, kernel):
    flipped = kernel[::-1, ::-1, ::-1]
    return lax.conv_general_dilated(grads, flipped, (1, 1, 1), ((1, 2), (1, 2), (1, 2)), lhs_dilation=(2, 2, 2), dimension_numbers=('NDHWC', 'DHWOI', 'NDHWC'), precision=lax.Precision.HIGHEST, preferred_element_type=jnp.float32)

def pad_low(field):
    return jnp.pad(field, ((0, 0), (1, 0), (1, 0), (1, 0), (0, 0)))

def reference(volume, kernel_a, kernel_b, cotangent):
    weights_a = kernel_a.astype(jnp.float32)
    weights_b = kernel_b.astype(jnp.float32)

    def one_sample(carry, items):
        sample, grads = items
        field = sample.astype(jnp.float32).reshape(1, GRID, GRID, GRID, C0)
        padded_x = pad_low(field)
        pre = forward_conv(padded_x, weights_a)
        hidden = lax.optimization_barrier(jnp.where(pre > 0, pre, 0.3 * pre).astype(jnp.bfloat16))
        padded_h = pad_low(hidden.astype(jnp.float32))
        output = forward_conv(padded_h, weights_b).astype(jnp.bfloat16)
        upstream = grads.astype(jnp.float32)[None]
        part_b = kernel_grad(padded_h, upstream)
        back = lax.optimization_barrier(input_grad(upstream, weights_b).astype(jnp.bfloat16))
        delta = lax.optimization_barrier((back.astype(jnp.float32) * jnp.where(pre > 0, 1.0, 0.3)).astype(jnp.bfloat16))
        part_a = kernel_grad(padded_x, delta.astype(jnp.float32))
        return ((carry[0] + part_a, carry[1] + part_b), output[0])
    start = (jnp.zeros((3, 3, 3, C0, C1), jnp.float32), jnp.zeros((3, 3, 3, C1, C2), jnp.float32))
    totals, features = lax.scan(one_sample, start, (volume, cotangent))
    grad_a = totals[0] / math.sqrt(SAMPLES * (GRID // 2) ** 3)
    grad_b = totals[1] / math.sqrt(SAMPLES * (GRID // 4) ** 3)
    return (features, grad_a, grad_b)
```

```python
import functools
import math

import jax
import jax.numpy as jnp
from jax import lax
from jax.experimental import pallas as pl
from jax.experimental.pallas import tpu as pltpu
from jax.sharding import PartitionSpec as P

GRID = 64
BF = jnp.bfloat16
F32 = jnp.float32
VMEM = pl.BlockSpec(memory_space=pltpu.VMEM)
TAPS = 27
PAIRS = 5
MIB = 1 << 20


def dot(a, b):
    return lax.dot_general(a, b, (((1,), (0,)), ((), ())), preferred_element_type=F32)


def dot_nt(a, b):
    return lax.dot_general(a, b, (((1,), (1,)), ((), ())), preferred_element_type=F32)


def iota(shape, dim):
    return lax.broadcasted_iota(jnp.int32, shape, dim)


def params(mib=48):
    return pltpu.CompilerParams(vmem_limit_bytes=mib * MIB)


def deinterleave(x):
    row = iota((80, 64), 0)
    col = iota((80, 64), 1)
    pick = (col == 4 * (row % 16) + row // 16 - 1).astype(F32).astype(BF)
    return dot(pick, x).astype(BF)


def store_plane(ref, plane, x):
    y = deinterleave(x)
    for slot in range(5):
        ref[plane, slot, 0:16, :] = jnp.zeros((16, 256), BF)
        for s in range(8):
            ref[plane, slot, 16 + 16 * s : 32 + 16 * s, :] = y[
                16 * slot : 16 * slot + 16, 256 * s : 256 * s + 256
            ]


def build_first(ka_ref, ta_ref):
    left = iota((32, 128), 1) < 64
    zero = jnp.zeros((32, 128), F32)
    for t in range(9):
        wide = []
        for c in range(3):
            k = ka_ref[t // 3, t % 3, c].astype(F32)
            wide.append(jnp.concatenate([k, k], axis=1))
        for half in range(2):
            for w in range(-4, 8):
                row = 384 * t + (32 * w if w >= 0 else 256 + 32 * (w + 4))
                c0 = w - 4 * half + 1
                c1 = c0 - 2
                l = wide[c0] if 0 <= c0 <= 2 else zero
                r = wide[c1] if 0 <= c1 <= 2 else zero
                ta_ref[row : row + 32, 128 * half : 128 * half + 128] = jnp.where(left, l, r).astype(BF)


def first_rows(plane, b):
    main = jnp.concatenate([plane(b, 16, 0, 256), plane(b + 2, 16, 0, 256)], axis=0)
    edge = jnp.concatenate([plane(b, 0, 128, 128), plane(b + 2, 0, 128, 128)], axis=0)
    return [main, edge]


def first_conv(planes, ta_ref):
    total = None
    for a in range(3):
        parts = []
        for b in range(3):
            parts += first_rows(planes[a], b)
        term = dot(jnp.concatenate(parts, axis=1), ta_ref[1152 * a : 1152 * a + 1152, :])
        total = term if total is None else total + term
    return total


def down_shift(x):
    moved = pltpu.roll(x, 1, 0)
    return jnp.where(iota(x.shape, 0) % 16 == 0, 0.0, moved)


def up_shift(x):
    moved = pltpu.roll(x, x.shape[0] - 1, 0)
    return jnp.where(iota(x.shape, 0) % 16 == 15, 0.0, moved)


def store_hidden(put, even, odd):
    put(0, down_shift(odd).astype(BF))
    put(1, even.astype(BF))
    put(2, odd.astype(BF))


def leaky(pre):
    return jnp.where(pre > 0, pre, 0.3 * pre)


def sub(ref, *lead):
    def read(slot, row, lane, width):
        return ref[(*lead, slot, slice(row, row + 128), slice(lane, lane + width))]

    return read


def first_kernel(vol_ref, ka_ref, vd_ref, h_ref, ta_ref, last_ref):
    step = pl.program_id(0)

    @pl.when(step == 0)
    def _():
        build_first(ka_ref, ta_ref)

    for k in range(2):
        store_plane(vd_ref, k, vol_ref[0, k])

    @pl.when(step > 0)
    def _():
        hid = leaky(first_conv([sub(last_ref), sub(vd_ref, 0), sub(vd_ref, 1)], ta_ref))

        def put(slot, x):
            h_ref[0, slot, 0:16, :] = jnp.zeros((16, 256), BF)
            h_ref[0, slot, 16:144, :] = x

        store_hidden(put, hid[0:128], hid[128:256])

    last_ref[...] = vd_ref[1]


def pack_kernel(n, cot_ref, out_ref):
    chan = cot_ref.shape[4]
    lanes = 128 // chan
    rows = 256 // lanes
    per = 16 // n
    row = iota((256, 256), 0)
    col = iota((256, 256), 1)
    source = (row % 16) * 16 + ((row % rows) // 16) * lanes + row // rows
    pick = (col == source).astype(F32).astype(BF)
    for p in range(16):
        y = dot(pick, cot_ref[0, p].reshape(256, chan))
        z = jnp.concatenate([y[rows * l : rows * l + rows] for l in range(lanes)], axis=1).astype(BF)
        t = p // per
        at = (p % per) * rows
        out_ref[t, at : at + rows, :] = z
        if p % per == 0 and t > 0:
            out_ref[t - 1, per * rows : per * rows + rows, :] = z
    out_ref[n - 1, per * rows : per * rows + rows, :] = jnp.zeros((rows, 128), BF)


def lane_order(n, inverse):
    size = n * 128
    chan = 128 // n
    row = iota((size, size), 0)
    col = iota((size, size), 1)
    if inverse:
        row, col = col, row
    target = ((row // chan) % n) * 128 + (row // 128) * chan + row % chan
    return (col == target).astype(F32).astype(BF)


def second_rows(hread, a, count):
    parts = []
    for b in range(3):
        parts.append(jnp.concatenate([hread(2 * p + a, b, 16, 0, 256) for p in range(count)], axis=0))
        parts.append(jnp.concatenate([hread(2 * p + a, b, 0, 128, 128) for p in range(count)], axis=0))
    return jnp.concatenate(parts, axis=1)


def hidden_reader(h_ref, h0_ref, hh_ref):
    def read(index, slot, row, lane, width):
        rows, cols = slice(row, row + 128), slice(lane, lane + width)
        if index == 0:
            return hh_ref[slot, rows, cols]
        if index == 1:
            return h0_ref[slot, rows, cols]
        return h_ref[index - 1, slot, rows, cols]

    return read


def grad_b_kernel(
    n, dp, halo_ref, ka_ref, vd_ref, h_ref, hrecv_ref, cot_ref, vdh_ref, h0_ref, hh_ref, c_ref, out_ref, ta_ref
):
    slab = 16 // n
    chan = 64 // n
    lanes = n
    rows = 256 // lanes
    build_first(ka_ref, ta_ref)
    x = halo_ref[...].reshape(64, 2048)
    y = deinterleave(x)
    for slot in range(5):
        vdh_ref[slot, 0:16, :] = jnp.zeros((16, 256), BF)
        for s in range(8):
            vdh_ref[slot, 16 + 16 * s : 32 + 16 * s, :] = y[16 * slot : 16 * slot + 16, 256 * s : 256 * s + 256]
    hid = leaky(first_conv([sub(vdh_ref), sub(vd_ref, 0), sub(vd_ref, 1)], ta_ref))

    def put_in(ref):
        def put(slot, v):
            ref[slot, 0:16, :] = jnp.zeros((16, 256), BF)
            ref[slot, 16:144, :] = v

        return put

    store_hidden(put_in(h0_ref), hid[0:128], hid[128:256])
    store_hidden(put_in(hh_ref), hrecv_ref[0].astype(F32), hrecv_ref[1].astype(F32))
    wide = jnp.concatenate([cot_ref[t] for t in range(n)], axis=1)
    turned = dot(wide, lane_order(n, False))
    mains = []
    for p in range(slab + 1):
        main = jnp.concatenate(
            [
                turned[
                    p * rows + 16 * (2 * s // lanes) : p * rows + 16 * (2 * s // lanes) + 16,
                    128 * (2 * s % lanes) : 128 * (2 * s % lanes) + 256,
                ]
                for s in range(8)
            ],
            axis=0,
        )
        mains.append(main)
        for slot, v in enumerate((main, up_shift(main))):
            c_ref[p, slot, 0:128, :] = v.astype(BF)
            c_ref[p, slot, 128:144, :] = jnp.zeros((16, 256), BF)
    turn = jnp.concatenate(mains[:slab], axis=0).T.astype(BF)
    read = hidden_reader(h_ref, h0_ref, hh_ref)
    per = 32 // dp
    out_ref[...] = jnp.zeros(out_ref.shape, BF)

    def put_tap(tap, v):
        v = v.astype(BF)
        for z in range(n):
            at = (tap % per) * chan
            out_ref[(tap // per) * n + z, at : at + chan, :] = v[z * chan : z * chan + chan]

    for a in range(3):
        g = dot(turn, second_rows(read, a, slab))
        for b in range(3):
            t = 3 * a + b
            l = 384 * b
            one = (g[0:128, l : l + 128] + g[128:256, l + 128 : l + 256]).T
            two = (g[0:128, l + 256 : l + 384] + g[128:256, l : l + 128]).T
            put_tap(3 * t, two[64:128])
            put_tap(3 * t + 1, one[0:64])
            put_tap(3 * t + 2, one[64:128])


def second_kernel(n, kb_ref, h_ref, h0_ref, hh_ref, c_ref, vd_ref, vdh_ref, feat_ref, out_ref, tb_ref, d_ref):
    slab = 16 // n
    planes = 2 * slab
    chan = 64 // n
    lanes = n
    rows = 256 // lanes
    blank = jnp.zeros((64, 128), BF)
    for t in range(9):
        taps = []
        for c in range(3):
            at = (3 * t + c) * chan
            taps.append(jnp.concatenate([kb_ref[z, at : at + chan, :] for z in range(n)], axis=0))
        for w in range(-2, 4):
            row = 384 * t + (64 * w if w >= 0 else 256 + 64 * (w + 2))
            for r in range(2):
                c = w - 2 * r + 1
                tb_ref[row : row + 64, 128 * r : 128 * r + 128] = taps[c] if 0 <= c <= 2 else blank
    read = hidden_reader(h_ref, h0_ref, hh_ref)
    total = None
    for a in range(3):
        term = dot(second_rows(read, a, slab), tb_ref[1152 * a : 1152 * a + 1152, :])
        total = term if total is None else total + term
    total = total.astype(BF)
    wide = []
    for p in range(slab):
        for m in range(16 // lanes):
            at = 128 * p + 16 * (m * lanes // 2)
            wide.append(
                jnp.concatenate([total[at + 16 * k : at + 16 * k + 16] for k in range(lanes // 2)], axis=1)
            )
    packed = dot(jnp.concatenate(wide, axis=0), lane_order(n, True)).astype(BF)
    for z in range(n):
        feat_ref[z] = packed[:, 128 * z : 128 * z + 128]
    for par in range(2):
        for hp in range(2):
            low, high = None, None
            for a in (1,) if par == 0 else (0, 2):
                for b in (1,) if hp == 0 else (0, 2):
                    t = 3 * a + b
                    up = 1 if a == 0 else 0
                    slot = 1 if b == 0 else 0
                    main = jnp.concatenate([c_ref[p + up, slot, 0:128, :] for p in range(slab)], axis=0)
                    edge = jnp.concatenate([c_ref[p + up, slot, 16:144, 0:128] for p in range(slab)], axis=0)
                    x = dot_nt(main, tb_ref[384 * t : 384 * t + 256, :])
                    e = dot_nt(edge, tb_ref[384 * t + 256 : 384 * t + 384, 0:128])
                    low = x[:, 0:128] if low is None else low + x[:, 0:128]
                    high = x[:, 128:256] + e if high is None else high + x[:, 128:256] + e
            back = jnp.concatenate([low, high], axis=1).astype(BF).astype(F32)
            for p in range(slab):
                u = 2 * p + par
                mask = read(u + 1, 1 + hp, 16, 0, 256).astype(F32) > 0
                v = back[128 * p : 128 * p + 128]
                at = 256 * u + 128 * hp
                d_ref[:, at : at + 128] = jnp.where(mask, v, 0.3 * v).astype(BF).astype(F32).T.astype(BF)
    left = iota((64, 128), 1) < 32
    pieces = []
    for a in range(3):
        for b in range(3):
            mains, edges = [], []
            for u in range(planes):
                src = sub(vdh_ref) if 2 * u + a == 0 else sub(vd_ref, 2 * u + a - 1)
                m, e = first_rows(src, b)
                mains.append(m)
                edges.append(e)
            x = jnp.concatenate([jnp.concatenate(mains, axis=0), jnp.concatenate(edges, axis=0)], axis=1)
            g = dot(d_ref[...], x)
            one = g[0:64, 256:384] + g[128:192, 0:128]
            two = g[0:64, 0:128] + g[128:192, 128:256]
            three = g[64:128, 0:128] + g[192:256, 128:256]
            pieces.append(
                jnp.where(left, pltpu.roll(one, 32, 1), pltpu.roll(two, 32, 1)) + pltpu.roll(three, 96, 1)
            )
    pieces.append(jnp.zeros((64, 128), F32))
    out_ref[...] = jnp.zeros(out_ref.shape, BF)
    for k in range(PAIRS):
        both = jnp.concatenate([pieces[2 * k], pieces[2 * k + 1]], axis=0).T.astype(BF)
        for j in range(6):
            out_ref[6 * k + j] = both[16 * j : 16 * j + 16]


def sum_kernel(scale, in_ref, out_ref):
    total = in_ref[0].astype(F32)
    for k in range(1, in_ref.shape[0]):
        total = total + in_ref[k].astype(F32)
    total = total * scale
    for k in range(out_ref.shape[0]):
        out_ref[k] = total


def unpack_kernel(n, in_ref, out_ref):
    chan = out_ref.shape[4]
    lanes = 128 // chan
    rows = 256 // lanes
    per = 16 // n
    row = iota((256, 256), 0)
    col = iota((256, 256), 1)
    source = (col % 16) * 16 + ((col % rows) // 16) * lanes + col // rows
    pick = (row == source).astype(F32).astype(BF)
    for p in range(16):
        z = in_ref[p // per, (p % per) * rows : (p % per) * rows + rows, :].astype(F32)
        x = jnp.concatenate([z[:, chan * l : chan * l + chan] for l in range(lanes)], axis=0).astype(BF)
        out_ref[0, p] = dot(pick, x).astype(BF).reshape(16, 16, chan)


def last_kernel(in_ref, out_ref):
    for k in range(PAIRS):
        for c in range(3):
            x = jnp.concatenate([in_ref[6 * k + 2 * c], in_ref[6 * k + 2 * c + 1]], axis=0)
            for j in range(2):
                t = 2 * k + j
                if t < 9:
                    out_ref[t // 3, t % 3, c] = x[:, 64 * j : 64 * j + 64]


def call(body, outs, ins, scratch=(), mib=48):
    return pl.pallas_call(
        body,
        out_shape=outs,
        in_specs=[VMEM] * ins,
        out_specs=[VMEM] * len(outs) if isinstance(outs, (list, tuple)) else VMEM,
        scratch_shapes=list(scratch),
        compiler_params=params(mib),
    )


def shards(volume, kernel_a, kernel_b, cotangent):
    n = lax.axis_size("mp")
    dp = lax.axis_size("dp")
    both = ("dp", "mp")
    planes = volume.shape[1]
    hplanes = planes // 2
    slab = hplanes // 2
    chan_b = kernel_b.shape[3]
    chan_o = cotangent.shape[4]
    rows = 256 // (128 // chan_o)
    shape = jax.ShapeDtypeStruct
    up = [(i, i + 1) for i in range(n - 1)]

    halo = lax.ppermute(volume[0, planes - 1], "mp", up)
    packed = call(functools.partial(pack_kernel, n), shape((n, (slab + 1) * rows, 128), BF), 1)(cotangent)
    cot = lax.all_to_all(packed, "mp", 0, 0, tiled=True)
    kb = kernel_b.reshape(1, TAPS * chan_b, 128)
    kb = lax.all_to_all(jnp.broadcast_to(kb, (n, TAPS * chan_b, 128)), "mp", 0, 0, tiled=True)

    vd, hidden = pl.pallas_call(
        first_kernel,
        grid=(hplanes,),
        out_shape=(shape((planes, 5, 144, 256), BF), shape((hplanes, 3, 144, 256), BF)),
        in_specs=[pl.BlockSpec((1, 2, 64, 2048), lambda i: (0, i, 0, 0)), VMEM],
        out_specs=(
            pl.BlockSpec((2, 5, 144, 256), lambda i: (i, 0, 0, 0)),
            pl.BlockSpec((1, 3, 144, 256), lambda i: (i, 0, 0, 0)),
        ),
        scratch_shapes=[pltpu.VMEM((3456, 256), BF), pltpu.VMEM((5, 144, 256), BF)],
        compiler_params=params(),
    )(volume, kernel_a)
    hrecv = lax.ppermute(hidden[hplanes - 1, 1:3, 16:144, :], "mp", up)

    per = 32 // dp
    vdh, h0, hh, c, gb = call(
        functools.partial(grad_b_kernel, n, dp),
        (
            shape((5, 144, 256), BF),
            shape((3, 144, 256), BF),
            shape((3, 144, 256), BF),
            shape((slab + 1, 2, 144, 256), BF),
            shape((dp * n, per * chan_b, 128), BF),
        ),
        6,
        [pltpu.VMEM((3456, 256), BF)],
    )(halo, kernel_a, vd[0:2], hidden, hrecv, cot)
    gb = lax.all_to_all(gb, both, 0, 0, tiled=True)

    feat, ga = call(
        functools.partial(second_kernel, n),
        (shape((n, slab * rows, 128), BF), shape((dp * n, 16, 128), BF)),
        7,
        [pltpu.VMEM((3456, 256), BF), pltpu.VMEM((256, hplanes * 256), BF)],
    )(kb, hidden, h0, hh, c, vd, vdh)
    feat = lax.all_to_all(feat, "mp", 0, 0, tiled=True)
    ga = lax.all_to_all(ga, both, 0, 0, tiled=True)

    samples = volume.shape[0] * dp
    gb = call(
        functools.partial(sum_kernel, 1 / math.sqrt(samples * (GRID // 4) ** 3)),
        shape((dp, per * chan_b, 128), F32),
        1,
    )(gb)
    gb = lax.all_to_all(gb, "dp", 0, 0, tiled=True)
    ga = call(
        functools.partial(sum_kernel, 1 / math.sqrt(samples * (GRID // 2) ** 3)),
        shape((dp * n, 16, 128), F32),
        1,
    )(ga)
    ga = lax.all_to_all(ga, both, 0, 0, tiled=True)

    features = call(functools.partial(unpack_kernel, n), shape((1, 16, 16, 16, chan_o), BF), 1)(feat)
    grad_b = gb.reshape(32, chan_b, 128)[:TAPS].reshape(3, 3, 3, chan_b, 128)
    grad_a = call(last_kernel, shape((3, 3, 3, 32, 64), F32), 1)(ga)
    return (features, grad_a, grad_b)


def solution(mesh):
    return jax.shard_map(
        shards,
        mesh=mesh,
        in_specs=(
            P("dp", "mp", None, None),
            P(),
            P(None, None, None, "mp", None),
            P("dp", None, None, None, "mp"),
        ),
        out_specs=(P("dp", None, None, None, "mp"), P(), P(None, None, None, "mp", None)),
        check_vma=False,
    )
```

```python
import functools
import math

import jax
import jax.numpy as jnp
from jax import lax
from jax.experimental import pallas as pl
from jax.experimental.pallas import tpu as pltpu
from jax.sharding import PartitionSpec as P

GRID = 64
BF = jnp.bfloat16
F32 = jnp.float32
VMEM = pl.BlockSpec(memory_space=pltpu.VMEM)
TAPS = 27
HALF = 14
PAIRS = 5
MIB = 1 << 20


def dot(a, b):
    return lax.dot_general(a, b, (((1,), (0,)), ((), ())), preferred_element_type=F32)


def dot_nt(a, b):
    return lax.dot_general(a, b, (((1,), (1,)), ((), ())), preferred_element_type=F32)


def iota(shape, dim):
    return lax.broadcasted_iota(jnp.int32, shape, dim)


def params(mib):
    return pltpu.CompilerParams(vmem_limit_bytes=mib * MIB)


def cost(us):
    return pl.CostEstimate(flops=int(us * 1e9), bytes_accessed=int(us * 3e6), transcendentals=0)


def deinterleave(x, count):
    row = iota((80 * count, 64 * count), 0)
    col = iota((80 * count, 64 * count), 1)
    h = 4 * (row % 16) + row % 80 // 16 - 1
    pick = jnp.logical_and(h >= 0, col == row // 80 * 64 + h).astype(F32).astype(BF)
    return dot(pick, x).astype(BF)


def store_plane(ref, lead, y, row):
    for slot in range(5):
        ref[(*lead, slot, slice(0, 16))] = jnp.zeros((16, 256), BF)
        for s in range(8):
            at = row + 16 * slot
            ref[(*lead, slot, slice(16 + 16 * s, 32 + 16 * s))] = y[at : at + 16, 256 * s : 256 * s + 256]


def build_first(ka_ref, ta_ref, taps=9):
    left = iota((32, 128), 1) < 64
    zero = jnp.zeros((32, 128), F32)
    for t in range(taps):
        wide = []
        for c in range(3):
            k = ka_ref[t // 3, t % 3, c].astype(F32)
            wide.append(jnp.concatenate([k, k], axis=1))
        for half in range(2):
            for w in range(-4, 8):
                row = 384 * t + (32 * w if w >= 0 else 256 + 32 * (w + 4))
                c0 = w - 4 * half + 1
                c1 = c0 - 2
                l = wide[c0] if 0 <= c0 <= 2 else zero
                r = wide[c1] if 0 <= c1 <= 2 else zero
                ta_ref[row : row + 32, 128 * half : 128 * half + 128] = jnp.where(left, l, r).astype(BF)


def first_rows(plane, b):
    main = jnp.concatenate([plane(b, 16, 0, 256), plane(b + 2, 16, 0, 256)], axis=0)
    edge = jnp.concatenate([plane(b, 0, 128, 128), plane(b + 2, 0, 128, 128)], axis=0)
    return [main, edge]


def first_term(planes, a, ta_ref):
    parts = []
    for b in range(3):
        both = [first_rows(plane, b) for plane in planes]
        parts.append(jnp.concatenate([m for m, _ in both], axis=0))
        parts.append(jnp.concatenate([e for _, e in both], axis=0))
    return dot(jnp.concatenate(parts, axis=1), ta_ref[1152 * a : 1152 * a + 1152, :])


def down_shift(x):
    moved = pltpu.roll(x, 1, 0)
    return jnp.where(iota(x.shape, 0) % 16 == 0, 0.0, moved)


def up_shift(x):
    moved = pltpu.roll(x, x.shape[0] - 1, 0)
    return jnp.where(iota(x.shape, 0) % 16 == 15, 0.0, moved)


def store_hidden(put, even, odd):
    put(0, down_shift(odd).astype(BF))
    put(1, even.astype(BF))
    put(2, odd.astype(BF))


def leaky(pre):
    return jnp.where(pre > 0, pre, 0.3 * pre)


def sub(ref, *lead):
    def read(slot, row, lane, width):
        return ref[(*lead, slot, slice(row, row + 128), slice(lane, lane + width))]

    return read


def first_kernel(vol_ref, ka_ref, out_ref, hout_ref, pre_ref, x_ref, vd_ref, h_ref, ta_ref, sems, out_sems, h_sems):
    steps = x_ref.shape[0]

    def fetch(i):
        return pltpu.make_async_copy(vol_ref.at[0, pl.ds(4 * i, 4)], x_ref.at[i], sems.at[i])

    def flush(i):
        return pltpu.make_async_copy(
            vd_ref.at[pl.ds(4 * i + 1, 4)], out_ref.at[pl.ds(4 * i, 4)], out_sems.at[i]
        )

    def flush_hidden(i):
        return pltpu.make_async_copy(h_ref.at[pl.ds(2 * i, 2)], hout_ref.at[pl.ds(2 * i, 2)], h_sems.at[i])

    for i in range(steps):
        fetch(i).start()
    build_first(ka_ref, ta_ref)
    vd_ref[0] = jnp.zeros((5, 144, 256), BF)

    @pl.loop(0, steps)
    def _(i):
        fetch(i).wait()
        y = deinterleave(x_ref[i].reshape(256, 2048), 4)
        for k in range(4):
            store_plane(vd_ref, (4 * i + k + 1,), y, 80 * k)
        flush(i).start()
        total = None
        for a in range(3):
            term = first_term([sub(vd_ref, 4 * i + a), sub(vd_ref, 4 * i + a + 2)], a, ta_ref)
            total = term if total is None else total + term

        @pl.when(i == 0)
        def _():
            pre_ref[...] = total[0:256]

        hid = leaky(total)
        for k in range(2):

            def put(slot, x):
                h_ref[2 * i + k, slot, 0:16, :] = jnp.zeros((16, 256), BF)
                h_ref[2 * i + k, slot, 16:144, :] = x

            store_hidden(put, hid[256 * k : 256 * k + 128], hid[256 * k + 128 : 256 * k + 256])
        flush_hidden(i).start()

    for i in range(steps):
        flush(i).wait()
        flush_hidden(i).wait()


def core_of():
    return lax.axis_index("dp") % 2


def plane_kernel(vol_ref, out_ref, sem):
    copy = pltpu.make_async_copy(vol_ref.at[0, vol_ref.shape[1] - 1], out_ref, sem)
    copy.start()
    copy.wait()


def pack_kernel(n, cot_ref, kb_ref, after_ref, out_ref):
    del after_ref
    chan = cot_ref.shape[4]
    lanes = 128 // chan
    rows = 256 // lanes
    per = 16 // n
    row = iota((256, 256), 0)
    col = iota((256, 256), 1)
    source = (row % 16) * 16 + ((row % rows) // 16) * lanes + row // rows
    pick = (col == source).astype(F32).astype(BF)
    for p in range(16):
        y = dot(pick, cot_ref[0, p].reshape(256, chan))
        z = jnp.concatenate([y[rows * l : rows * l + rows] for l in range(lanes)], axis=1).astype(BF)
        t = p // per
        at = (p % per) * rows
        out_ref[t, at : at + rows, :] = z
        if p % per == 0 and t > 0:
            out_ref[t - 1, per * rows : per * rows + rows, :] = z
    out_ref[n - 1, per * rows : per * rows + rows, :] = jnp.zeros((rows, 128), BF)
    first = 13 * core_of()
    size = kb_ref.shape[1]
    for j in range(HALF):
        v = kb_ref[first + j]
        at = (per + 1) * rows + size * j
        for t in range(n):
            out_ref[t, at : at + size, :] = v


def lane_order(n, inverse):
    size = n * 128
    chan = 128 // n
    row = iota((size, size), 0)
    col = iota((size, size), 1)
    if inverse:
        row, col = col, row
    target = ((row // chan) % n) * 128 + (row // 128) * chan + row % chan
    return (col == target).astype(F32).astype(BF)


def second_rows(hread, a, count):
    planes = [2 * p + a - 1 for p in range(count + 1)][1 if a == 0 else 0 :][:count]
    parts = []
    for b in range(3):
        parts.append(jnp.concatenate([hread(u, b, 16, 0, 256) for u in planes], axis=0))
        parts.append(jnp.concatenate([hread(u, b, 0, 128, 128) for u in planes], axis=0))
    return jnp.concatenate(parts, axis=1)


def hidden_reader(h_ref, h0_ref):
    def read(index, slot, row, lane, width):
        rows, cols = slice(row, row + 128), slice(lane, lane + width)
        return h0_ref[slot, rows, cols] if index == 0 else h_ref[index, slot, rows, cols]

    return read


def put_in(ref):
    def put(slot, v):
        ref[slot, 0:16, :] = jnp.zeros((16, 256), BF)
        ref[slot, 16:144, :] = v

    return put


def put_half(keep_ref, send_ref, item, v):
    mine = core_of() == item % 2

    @pl.when(mine)
    def _():
        keep_ref[item // 2] = v

    @pl.when(jnp.logical_not(mine))
    def _():
        send_ref[item // 2] = v


def clear_from(count, keep_ref, send_ref):
    zero = jnp.zeros(keep_ref.shape[1:], F32)
    for item in range(count, 2 * keep_ref.shape[0]):
        put_half(keep_ref, send_ref, item, zero)


def grad_b_kernel(
    n, halo_ref, ka_ref, pre_ref, hin_ref, cot_ref, vdh_ref, h0_ref, c_ref, keep_ref, send_ref, ta_ref, h_ref, sem
):
    fetch = pltpu.make_async_copy(hin_ref, h_ref, sem)
    fetch.start()
    slab = 16 // n
    lanes = n
    rows = 256 // lanes
    build_first(ka_ref, ta_ref, 3)
    store_plane(vdh_ref, (), deinterleave(halo_ref[...], 1), 0)
    hid = leaky(pre_ref[...] + first_term([sub(vdh_ref)], 0, ta_ref))
    store_hidden(put_in(h0_ref), hid[0:128], hid[128:256])
    wide = jnp.concatenate([cot_ref[t, 0 : (slab + 1) * rows, :] for t in range(n)], axis=1)
    turned = dot(wide, lane_order(n, False))
    turns = []
    for p in range(slab + 1):
        main = jnp.concatenate(
            [
                turned[
                    p * rows + 16 * (2 * s // lanes) : p * rows + 16 * (2 * s // lanes) + 16,
                    128 * (2 * s % lanes) : 128 * (2 * s % lanes) + 256,
                ]
                for s in range(8)
            ],
            axis=0,
        )
        turns.append(main.T.astype(BF))
        for slot, v in enumerate((main, up_shift(main))):
            c_ref[p, slot, 0:128, :] = v.astype(BF)
            c_ref[p, slot, 128:144, :] = jnp.zeros((16, 256), BF)
    read = hidden_reader(h_ref, h0_ref)
    clear_from(TAPS, keep_ref, send_ref)
    fetch.wait()
    for a in range(3):
        first = 1 if a == 0 else 0
        turn = jnp.concatenate(turns[first : first + slab], axis=1)
        g = dot(turn, second_rows(read, a, slab))
        for b in range(3):
            t = 3 * a + b
            l = 384 * b
            one = (g[0:128, l : l + 128] + g[128:256, l + 128 : l + 256]).T
            two = (g[0:128, l + 256 : l + 384] + g[128:256, l : l + 128]).T
            put_half(keep_ref, send_ref, 3 * t, two[64:128])
            put_half(keep_ref, send_ref, 3 * t + 1, one[0:64])
            put_half(keep_ref, send_ref, 3 * t + 2, one[64:128])


def build_second(n, kb_ref, other_ref, tb_ref):
    chan = 64 // n
    start = (16 // n + 1) * (256 // n)
    blank = jnp.zeros((64, 128), BF)
    first = core_of() == 0

    def tap(k):
        j, own_first = (k, True) if k < 13 else (k - 13, False)
        parts = []
        for z in range(n):
            own = kb_ref[z, start + j * chan : start + j * chan + chan, :]
            other = other_ref[z, start + j * chan : start + j * chan + chan, :]
            pair = (own, other) if own_first else (other, own)
            parts.append(jnp.where(first, *pair))
        return jnp.concatenate(parts, axis=0)

    for t in range(9):
        taps = [tap(3 * t + c) for c in range(3)]
        for w in range(-2, 4):
            row = 384 * t + (64 * w if w >= 0 else 256 + 64 * (w + 2))
            for r in range(2):
                c = w - 2 * r + 1
                tb_ref[row : row + 64, 128 * r : 128 * r + 128] = taps[c] if 0 <= c <= 2 else blank


def grad_a_kernel(n, kb_ref, other_ref, h_ref, h0_ref, c_ref, vd_ref, vdh_ref, keep_ref, send_ref, tb_ref, d_ref):
    slab = 16 // n
    planes = 2 * slab
    build_second(n, kb_ref, other_ref, tb_ref)
    read = hidden_reader(h_ref, h0_ref)
    for par in range(2):
        for hp in range(2):
            low, high = None, None
            for a in (1,) if par == 0 else (0, 2):
                for b in (1,) if hp == 0 else (0, 2):
                    t = 3 * a + b
                    up = 1 if a == 0 else 0
                    slot = 1 if b == 0 else 0
                    main = jnp.concatenate([c_ref[p + up, slot, 0:128, :] for p in range(slab)], axis=0)
                    edge = jnp.concatenate([c_ref[p + up, slot, 16:144, 0:128] for p in range(slab)], axis=0)
                    x = dot_nt(main, tb_ref[384 * t : 384 * t + 256, :])
                    e = dot_nt(edge, tb_ref[384 * t + 256 : 384 * t + 384, 0:128])
                    low = x[:, 0:128] if low is None else low + x[:, 0:128]
                    high = x[:, 128:256] + e if high is None else high + x[:, 128:256] + e
            back = jnp.concatenate([low, high], axis=1).astype(BF).astype(F32)
            for p in range(slab):
                u = 2 * p + par
                mask = read(u, 1 + hp, 16, 0, 256).astype(F32) > 0
                v = back[128 * p : 128 * p + 128]
                at = 256 * u + 128 * hp
                d_ref[:, at : at + 128] = jnp.where(mask, v, 0.3 * v).astype(BF).astype(F32).T.astype(BF)
    left = iota((64, 128), 1) < 32
    pieces = []
    for a in range(3):
        for b in range(3):
            mains, edges = [], []
            for u in range(planes):
                src = sub(vdh_ref) if 2 * u + a == 0 else sub(vd_ref, 2 * u + a - 1)
                m, e = first_rows(src, b)
                mains.append(m)
                edges.append(e)
            x = jnp.concatenate([jnp.concatenate(mains, axis=0), jnp.concatenate(edges, axis=0)], axis=1)
            g = dot(d_ref[...], x)
            one = g[0:64, 256:384] + g[128:192, 0:128]
            two = g[0:64, 0:128] + g[128:192, 128:256]
            three = g[64:128, 0:128] + g[192:256, 128:256]
            pieces.append(
                jnp.where(left, pltpu.roll(one, 32, 1), pltpu.roll(two, 32, 1)) + pltpu.roll(three, 96, 1)
            )
    pieces.append(jnp.zeros((64, 128), F32))
    clear_from(6 * PAIRS, keep_ref, send_ref)
    for k in range(PAIRS):
        both = jnp.concatenate([pieces[2 * k], pieces[2 * k + 1]], axis=0).T
        for j in range(6):
            put_half(keep_ref, send_ref, 6 * k + j, both[16 * j : 16 * j + 16])


def features_kernel(n, kb_ref, other_ref, h_ref, h0_ref, *refs):
    outs, (piece_ref, tb_ref) = refs[:n], refs[n:]
    slab = 16 // n
    lanes = n
    build_second(n, kb_ref, other_ref, tb_ref)
    read = hidden_reader(h_ref, h0_ref)
    terms = [dot(second_rows(read, a, slab), tb_ref[1152 * a : 1152 * a + 1152, :]) for a in range(3)]
    local = terms[1] + terms[2]
    total = jnp.concatenate(
        [local[0:128], local[128:] + terms[0][: 128 * slab - 128], terms[0][128 * slab - 128 :]], axis=0
    ).astype(BF)
    wide = []
    for p in range(slab + 1):
        for m in range(16 // lanes):
            at = 128 * p + 16 * (m * lanes // 2)
            wide.append(
                jnp.concatenate([total[at + 16 * k : at + 16 * k + 16] for k in range(lanes // 2)], axis=1)
            )
    packed = dot(jnp.concatenate(wide, axis=0), lane_order(n, True)).astype(BF)
    for z in range(n):
        piece_ref[z] = packed[:, 128 * z : 128 * z + 128]
    me = lax.axis_index("mp")
    for d in range(n):
        outs[d][...] = piece_ref[(me + d) % n]


def pair_kernel(keep_b, got_b, keep_a, got_a, out_ref):
    out_ref[:, 0:64, :] = (keep_b[...] + got_b[...]).astype(BF)
    out_ref[:, 64:80, :] = (keep_a[...] + got_a[...]).astype(BF)


def sum_kernel(n, scale_a, scale_b, in_ref, out_ref):
    chan = 64 // n
    total = in_ref[0].astype(F32)
    for k in range(1, in_ref.shape[0]):
        total = total + in_ref[k].astype(F32)
    tap = total[0:64] * scale_b
    rest = total[64:80] * scale_a
    for g in range(out_ref.shape[0]):
        z = g % n
        out_ref[g, 0:chan, :] = tap[z * chan : z * chan + chan].astype(BF)
        out_ref[g, chan : chan + 16, :] = rest.astype(BF)


def unpack_kernel(n, *refs):
    ins, out_ref = refs[:n], refs[n]
    chan = out_ref.shape[4]
    lanes = 128 // chan
    rows = 256 // lanes
    per = 16 // n
    row = iota((256, 256), 0)
    col = iota((256, 256), 1)
    source = (col % 16) * 16 + ((col % rows) // 16) * lanes + col // rows
    pick = (row == source).astype(F32).astype(BF)
    me = lax.axis_index("mp")
    for d in range(n):
        first = (me + n - d) % n * per
        for p in range(per):
            z = ins[d][p * rows : p * rows + rows, :].astype(F32)
            if p == 0:
                more = ins[(d + 1) % n][per * rows : per * rows + rows, :].astype(F32)
                z = z + jnp.where(first > 0, more, 0.0)
            x = jnp.concatenate([z[:, chan * l : chan * l + chan] for l in range(lanes)], axis=0).astype(BF)
            out_ref[0, first + p] = dot(pick, x).astype(BF).reshape(16, 16, chan)


def last_kernel(mine_ref, other_ref, a_ref, b_ref):
    chan = b_ref.shape[1]
    first = core_of() == 0
    for j in range(15):
        x, y = mine_ref[j].astype(F32), other_ref[j].astype(F32)
        x, y = jnp.where(first, x, y), jnp.where(first, y, x)
        if 2 * j < TAPS:
            b_ref[2 * j] = x[0:chan]
        if 2 * j + 1 < TAPS:
            b_ref[2 * j + 1] = y[0:chan]
        v = jnp.concatenate([x[chan : chan + 16], y[chan : chan + 16]], axis=0)
        for half in range(2):
            t = 2 * (j // 3) + half
            if t < 9:
                a_ref[t // 3, t % 3, j % 3] = v[:, 64 * half : 64 * half + 64]


def call(body, outs, ins, us, scratch=(), mib=16):
    return pl.pallas_call(
        body,
        out_shape=outs,
        grid=(1,),
        in_specs=[VMEM] * ins if isinstance(ins, int) else ins,
        out_specs=[VMEM] * len(outs) if isinstance(outs, (list, tuple)) else VMEM,
        scratch_shapes=list(scratch),
        compiler_params=params(mib),
        cost_estimate=cost(us),
    )


def shards(volume, kernel_a, kernel_b, cotangent):
    n = lax.axis_size("mp")
    dp = lax.axis_size("dp")
    planes = volume.shape[1]
    hplanes = planes // 2
    slab = hplanes // 2
    chan_b = kernel_b.shape[3]
    chan_o = cotangent.shape[4]
    rows = 256 // (128 // chan_o)
    shape = jax.ShapeDtypeStruct
    up = [(i, i + 1) for i in range(n - 1)]
    swap = [(i, i ^ 1) for i in range(dp)]
    groups = [[(2 * k + c) * n + z for k in range(dp // 2) for z in range(n)] for c in range(2)]
    peers = dp * n // 2

    def exchange(x):
        return lax.all_to_all(x, ("dp", "mp"), 0, 0, tiled=True, axis_index_groups=groups)

    volume, cotangent, kernel_b = (
        pltpu.with_memory_space_constraint(x, pltpu.HBM) for x in (volume, cotangent, kernel_b.reshape(TAPS, chan_b, 128))
    )
    sent = (slab + 1) * rows + HALF * chan_b
    halo = pl.pallas_call(
        plane_kernel,
        out_shape=pltpu.VMEM((64, 2048), BF),
        in_specs=[pl.BlockSpec(memory_space=pltpu.HBM)],
        out_specs=VMEM,
        scratch_shapes=[pltpu.SemaphoreType.DMA],
        compiler_params=params(2),
        cost_estimate=cost(1),
    )(volume)
    packed = pl.pallas_call(
        functools.partial(pack_kernel, n),
        grid=(1,),
        out_shape=shape((n, sent, 128), BF),
        in_specs=[
            pl.BlockSpec(cotangent.shape, lambda i: (0, 0, 0, 0, 0)),
            pl.BlockSpec((TAPS, chan_b, 128), lambda i: (0, 0, 0)),
            pl.BlockSpec(memory_space=pl.ANY),
        ],
        out_specs=pl.BlockSpec((n, sent, 128), lambda i: (0, 0, 0)),
        compiler_params=params(8),
        cost_estimate=cost(2),
    )(cotangent, kernel_b, halo)
    halo = lax.ppermute(halo, "mp", up)
    cot = lax.all_to_all(packed, "mp", 0, 0, tiled=True)
    vd, hidden, pre = pl.pallas_call(
        first_kernel,
        out_shape=(
            pltpu.HBM((planes, 5, 144, 256), BF),
            pltpu.HBM((hplanes, 3, 144, 256), BF),
            pltpu.VMEM((256, 256), F32),
        ),
        in_specs=[pl.BlockSpec(memory_space=pltpu.HBM), VMEM],
        out_specs=(pl.BlockSpec(memory_space=pltpu.HBM), pl.BlockSpec(memory_space=pltpu.HBM), VMEM),
        scratch_shapes=[
            pltpu.VMEM((planes // 4, 4, 64, 2048), BF),
            pltpu.VMEM((planes + 1, 5, 144, 256), BF),
            pltpu.VMEM((hplanes, 3, 144, 256), BF),
            pltpu.VMEM((3456, 256), BF),
            pltpu.SemaphoreType.DMA((planes // 4,)),
            pltpu.SemaphoreType.DMA((planes // 4,)),
            pltpu.SemaphoreType.DMA((planes // 4,)),
        ],
        compiler_params=params(24),
        cost_estimate=cost(100),
    )(volume, kernel_a)
    cot, pre, halo = lax.optimization_barrier((cot, pre, halo))
    kb_other = lax.ppermute(cot, "dp", swap)

    vdh, h0, c, keep_b, send_b = call(
        functools.partial(grad_b_kernel, n),
        (
            pltpu.VMEM((5, 144, 256), BF),
            pltpu.VMEM((3, 144, 256), BF),
            pltpu.VMEM((slab + 1, 2, 144, 256), BF),
            pltpu.VMEM((peers, 64, 128), F32),
            pltpu.VMEM((peers, 64, 128), F32),
        ),
        [VMEM, VMEM, VMEM, pl.BlockSpec(memory_space=pltpu.HBM), VMEM],
        3,
        [pltpu.VMEM((1152, 256), BF), pltpu.VMEM((hplanes, 3, 144, 256), BF), pltpu.SemaphoreType.DMA],
        16,
    )(halo, kernel_a, pre, pltpu.with_memory_space_constraint(hidden, pltpu.HBM), cot)
    got_b = lax.ppermute(send_b, "dp", swap)

    keep_a, send_a = call(
        functools.partial(grad_a_kernel, n),
        (shape((peers, 16, 128), F32), shape((peers, 16, 128), F32)),
        7,
        8,
        [pltpu.VMEM((3456, 256), BF), pltpu.VMEM((256, hplanes * 256), BF)],
        24,
    )(cot, kb_other, hidden, h0, c, vd, vdh)
    got_a = lax.ppermute(send_a, "dp", swap)

    sums = call(pair_kernel, shape((peers, 80, 128), BF), 4, 1)(keep_b, got_b, keep_a, got_a)
    sums = exchange(sums)

    pieces = call(
        functools.partial(features_kernel, n),
        [shape(((slab + 1) * rows, 128), BF)] * n,
        4,
        4,
        [
            pltpu.VMEM((n, (slab + 1) * rows, 128), BF),
            pltpu.VMEM((3456, 256), BF),
        ],
    )(cot, kb_other, hidden, h0)
    sums, *pieces = lax.optimization_barrier((sums, *pieces))
    pieces = [pieces[0]] + [
        lax.ppermute(pieces[d], "mp", [(i, (i + d) % n) for i in range(n)]) for d in range(1, n)
    ]

    samples = volume.shape[0] * dp
    scale_a = 1 / math.sqrt(samples * (GRID // 2) ** 3)
    scale_b = 1 / math.sqrt(samples * (GRID // 4) ** 3)
    mine = call(
        functools.partial(sum_kernel, n, scale_a, scale_b), shape((peers, chan_b + 16, 128), BF), 1, 1
    )(sums)
    mine = exchange(mine)
    mine, *pieces = lax.optimization_barrier((mine, *pieces))
    other = lax.ppermute(mine, "dp", swap)

    features = call(functools.partial(unpack_kernel, n), shape((1, 16, 16, 16, chan_o), BF), n, 2)(*pieces)
    grad_a, grad_b = call(
        last_kernel, (shape((3, 3, 3, 32, 64), F32), shape((TAPS, chan_b, 128), F32)), 2, 1
    )(mine, other)
    return (features, grad_a, grad_b.reshape(3, 3, 3, chan_b, 128))


def solution(mesh):
    return jax.shard_map(
        shards,
        mesh=mesh,
        in_specs=(
            P("dp", "mp", None, None),
            P(),
            P(None, None, None, "mp", None),
            P("dp", None, None, None, "mp"),
        ),
        out_specs=(P("dp", None, None, None, "mp"), P(), P(None, None, None, "mp", None)),
        check_vma=False,
    )
```

```python
import functools
import math

import jax
import jax.numpy as jnp
from jax import lax
from jax.experimental import pallas as pl
from jax.experimental.pallas import tpu as pltpu
from jax.sharding import PartitionSpec as P

GRID = 64
BF = jnp.bfloat16
F32 = jnp.float32
VMEM = pl.BlockSpec(memory_space=pltpu.VMEM)
TAPS = 27
HALF = 14
PAIRS = 5
MIB = 1 << 20


def dot(a, b):
    return lax.dot_general(a, b, (((1,), (0,)), ((), ())), preferred_element_type=F32)


def iota(shape, dim):
    return lax.broadcasted_iota(jnp.int32, shape, dim)


def params(mib):
    return pltpu.CompilerParams(vmem_limit_bytes=mib * MIB)


def cost(us):
    return pl.CostEstimate(flops=int(us * 1e9), bytes_accessed=int(us * 3e6), transcendentals=0)


def deinterleave(x, count):
    row = iota((80 * count, 64 * count), 0)
    col = iota((80 * count, 64 * count), 1)
    h = 4 * (row % 16) + row % 80 // 16 - 1
    pick = jnp.logical_and(h >= 0, col == row // 80 * 64 + h).astype(F32).astype(BF)
    return dot(pick, x).astype(BF)


def store_plane(ref, lead, y, row):
    for slot in range(5):
        ref[(*lead, slot, slice(0, 16))] = jnp.zeros((16, 256), BF)
        for s in range(8):
            at = row + 16 * slot
            ref[(*lead, slot, slice(16 + 16 * s, 32 + 16 * s))] = y[at : at + 16, 256 * s : 256 * s + 256]


def build_first(ka_ref, ta_ref, taps=9):
    left = iota((32, 128), 1) < 64
    zero = jnp.zeros((32, 128), F32)
    for t in range(taps):
        wide = []
        for c in range(3):
            k = ka_ref[t // 3, t % 3, c].astype(F32)
            wide.append(jnp.concatenate([k, k], axis=1))
        for half in range(2):
            for w in range(-4, 8):
                row = 384 * t + (32 * w if w >= 0 else 256 + 32 * (w + 4))
                c0 = w - 4 * half + 1
                c1 = c0 - 2
                l = wide[c0] if 0 <= c0 <= 2 else zero
                r = wide[c1] if 0 <= c1 <= 2 else zero
                ta_ref[row : row + 32, 128 * half : 128 * half + 128] = jnp.where(left, l, r).astype(BF)


def first_rows(plane, b):
    main = jnp.concatenate([plane(b, 16, 0, 256), plane(b + 2, 16, 0, 256)], axis=0)
    edge = jnp.concatenate([plane(b, 0, 128, 128), plane(b + 2, 0, 128, 128)], axis=0)
    return [main, edge]


def first_term(planes, a, ta_ref):
    parts = []
    for b in range(3):
        both = [first_rows(plane, b) for plane in planes]
        parts.append(jnp.concatenate([m for m, _ in both], axis=0))
        parts.append(jnp.concatenate([e for _, e in both], axis=0))
    return dot(jnp.concatenate(parts, axis=1), ta_ref[1152 * a : 1152 * a + 1152, :])


def down_shift(x):
    moved = pltpu.roll(x, 1, 0)
    return jnp.where(iota(x.shape, 0) % 16 == 0, 0.0, moved)


def next_group(x):
    moved = pltpu.roll(x, 112, 1)
    return jnp.where(iota(x.shape, 1) >= 112, 0.0, moved)


def up_shift(x):
    moved = pltpu.roll(x, x.shape[0] - 1, 0)
    return jnp.where(iota(x.shape, 0) % 16 == 15, 0.0, moved)


def store_hidden(put, even, odd):
    put(0, down_shift(odd).astype(BF))
    put(1, even.astype(BF))
    put(2, odd.astype(BF))


def leaky(pre):
    return jnp.where(pre > 0, pre, 0.3 * pre)


def sub(ref, *lead):
    def read(slot, row, lane, width):
        return ref[(*lead, slot, slice(row, row + 128), slice(lane, lane + width))]

    return read


def first_kernel(vol_ref, ka_ref, out_ref, h_ref, pre_ref, x_ref, vd_ref, ta_ref, sems, out_sems):
    steps = x_ref.shape[0]

    def fetch(i):
        return pltpu.make_async_copy(vol_ref.at[0, pl.ds(4 * i, 4)], x_ref.at[i], sems.at[i])

    def flush(i):
        return pltpu.make_async_copy(
            vd_ref.at[pl.ds(4 * i + 1, 4)], out_ref.at[pl.ds(4 * i, 4)], out_sems.at[i]
        )

    for i in range(steps):
        fetch(i).start()
    build_first(ka_ref, ta_ref)
    vd_ref[0] = jnp.zeros((5, 144, 256), BF)

    @pl.loop(0, steps)
    def _(i):
        fetch(i).wait()
        y = deinterleave(x_ref[i].reshape(256, 2048), 4)
        for k in range(4):
            store_plane(vd_ref, (4 * i + k + 1,), y, 80 * k)
        flush(i).start()
        total = None
        for a in range(3):
            term = first_term([sub(vd_ref, 4 * i + a), sub(vd_ref, 4 * i + a + 2)], a, ta_ref)
            total = term if total is None else total + term

        @pl.when(i == 0)
        def _():
            pre_ref[...] = total[0:256]

        hid = leaky(total)
        for k in range(2):

            def put(slot, x):
                h_ref[2 * i + k, slot, 0:16, :] = jnp.zeros((16, 256), BF)
                h_ref[2 * i + k, slot, 16:144, :] = x

            store_hidden(put, hid[256 * k : 256 * k + 128], hid[256 * k + 128 : 256 * k + 256])

    for i in range(steps):
        flush(i).wait()


def order(n):
    return sorted(range(n), key=lambda z: abs(2 * z - (n - 1)))


def place(n, z):
    return order(n).index(z)


def core_of():
    return lax.axis_index("dp") % 2


def plane_kernel(vol_ref, out_ref, sem):
    copy = pltpu.make_async_copy(vol_ref.at[0, vol_ref.shape[1] - 1], out_ref, sem)
    copy.start()
    copy.wait()


def pack_kernel(n, cot_ref, kb_ref, after_ref, out_ref):
    del after_ref
    chan = cot_ref.shape[4]
    lanes = 128 // chan
    rows = 256 // lanes
    per = 16 // n
    row = iota((256, 256), 0)
    col = iota((256, 256), 1)
    source = (row % 16) * 16 + ((row % rows) // 16) * lanes + row // rows
    pick = (col == source).astype(F32).astype(BF)
    for p in range(16):
        y = dot(pick, cot_ref[0, p].reshape(256, chan))
        z = jnp.concatenate([y[rows * l : rows * l + rows] for l in range(lanes)], axis=1).astype(BF)
        t = p // per
        at = (p % per) * rows
        out_ref[place(n, t), at : at + rows, :] = z
        if p % per == 0 and t > 0:
            out_ref[place(n, t - 1), per * rows : per * rows + rows, :] = z
    out_ref[place(n, n - 1), per * rows : per * rows + rows, :] = jnp.zeros((rows, 128), BF)
    first = 13 * core_of()
    size = kb_ref.shape[1]
    for j in range(HALF):
        v = kb_ref[first + j]
        at = (per + 1) * rows + size * j
        for t in range(n):
            out_ref[t, at : at + size, :] = v


def lane_order(n, inverse):
    size = n * 128
    chan = 128 // n
    row = iota((size, size), 0)
    col = iota((size, size), 1)
    if inverse:
        row, col = col, row
    target = ((row // chan) % n) * 128 + (row // 128) * chan + row % chan
    return (col == target).astype(F32).astype(BF)


def slab_planes(a, count):
    return [2 * p + a - 1 for p in range(count + 1)][1 if a == 0 else 0 :][:count]


def second_rows(hread, a, count):
    planes = slab_planes(a, count)
    parts = []
    for b in range(3):
        parts.append(jnp.concatenate([hread(u, b, 16, 0, 256) for u in planes], axis=0))
        parts.append(jnp.concatenate([hread(u, b, 0, 128, 128) for u in planes], axis=0))
    return jnp.concatenate(parts, axis=1)


def hidden_reader(h_ref, h0_ref):
    def read(index, slot, row, lane, width):
        rows, cols = slice(row, row + 128), slice(lane, lane + width)
        return h0_ref[slot, rows, cols] if index == 0 else h_ref[index, slot, rows, cols]

    return read


def put_in(ref):
    def put(slot, v):
        ref[slot, 0:16, :] = jnp.zeros((16, 256), BF)
        ref[slot, 16:144, :] = v

    return put


def put_half(both_ref, item, v):
    both_ref[(item + core_of()) % 2, item // 2] = v


def split_halves(count, both_ref, keep_ref, send_ref):
    zero = jnp.zeros(keep_ref.shape[1:], F32)
    for item in range(count, 2 * keep_ref.shape[0]):
        put_half(both_ref, item, zero)
    keep_ref[...] = both_ref[0]
    send_ref[...] = both_ref[1]


def halo_kernel(halo_ref, ka_ref, pre_ref, vd_out, h0_ref, vdh_ref, ta_ref, sem):
    build_first(ka_ref, ta_ref, 3)
    store_plane(vdh_ref, (), deinterleave(halo_ref[...], 1), 0)
    flush = pltpu.make_async_copy(vdh_ref, vd_out, sem)
    flush.start()
    hid = leaky(pre_ref[...] + first_term([sub(vdh_ref)], 0, ta_ref))
    store_hidden(put_in(h0_ref), hid[0:128], hid[128:256])
    flush.wait()


def grad_b_kernel(n, h_ref, h0_ref, cot_ref, c_ref, both_ref):
    slab = 16 // n
    lanes = n
    rows = 256 // lanes
    wide = jnp.concatenate([cot_ref[place(n, t), 0 : (slab + 1) * rows, :] for t in range(n)], axis=1)
    turned = dot(wide, lane_order(n, False))
    turns = []
    for p in range(slab + 1):
        main = jnp.concatenate(
            [
                turned[
                    p * rows + 16 * (2 * s // lanes) : p * rows + 16 * (2 * s // lanes) + 16,
                    128 * (2 * s % lanes) : 128 * (2 * s % lanes) + 256,
                ]
                for s in range(8)
            ],
            axis=0,
        )
        turn = main.T
        one = jnp.concatenate([turn[0:128], turn[128:256]], axis=1)
        two = jnp.concatenate([turn[128:256], next_group(turn[0:128])], axis=1)
        turns.append(jnp.concatenate([one, two], axis=0).astype(BF))
        for slot, v in enumerate((main, up_shift(main))):
            c_ref[p, slot, 0:128, :] = v.astype(BF)
            c_ref[p, slot, 128:144, :] = jnp.zeros((16, 256), BF)
    read = hidden_reader(h_ref, h0_ref)
    for a in range(3):
        first = 1 if a == 0 else 0
        turn = jnp.concatenate(turns[first : first + slab], axis=1)
        columns = []
        for b in range(3):
            tiles = [read(u, b, 16, 128 * k, 128) for u in slab_planes(a, slab) for k in range(2)]
            columns.append(jnp.concatenate(tiles, axis=0))
        g = dot(turn, jnp.concatenate(columns, axis=1))
        for b in range(3):
            t = 3 * a + b
            one = g[0:128, 128 * b : 128 * b + 128].T
            two = g[128:256, 128 * b : 128 * b + 128].T
            both_ref[3 * t % 2, 3 * t // 2] = two[64:128]
            both_ref[(3 * t + 1) % 2, (3 * t + 1) // 2] = one[0:64]
            both_ref[(3 * t + 2) % 2, (3 * t + 2) // 2] = one[64:128]
    for item in range(TAPS, 2 * both_ref.shape[1]):
        both_ref[item % 2, item // 2] = jnp.zeros(both_ref.shape[2:], F32)


def second_taps(n, kb_ref, other_ref):
    chan = 64 // n
    start = (16 // n + 1) * (256 // n)
    first = core_of() == 0

    def tap(k):
        j, own_first = (k, True) if k < 13 else (k - 13, False)
        parts = []
        for z in range(n):
            own = kb_ref[place(n, z), start + j * chan : start + j * chan + chan, :]
            other = other_ref[place(n, z), start + j * chan : start + j * chan + chan, :]
            pair = (own, other) if own_first else (other, own)
            parts.append(jnp.where(first, *pair))
        return jnp.concatenate(parts, axis=0)

    return tap


def build_second(n, kb_ref, other_ref, tb_ref):
    tap = second_taps(n, kb_ref, other_ref)
    blank = jnp.zeros((64, 128), BF)
    for t in range(9):
        taps = [tap(3 * t + c) for c in range(3)]
        for w in range(-2, 4):
            row = 384 * t + (64 * w if w >= 0 else 256 + 64 * (w + 2))
            for r in range(2):
                c = w - 2 * r + 1
                tb_ref[row : row + 64, 128 * r : 128 * r + 128] = taps[c] if 0 <= c <= 2 else blank


REACH = (((4,), (3, 5)), ((1, 7), (0, 2, 6, 8)))


def build_transposed(n, kb_ref, other_ref, tb_ref):
    tap = second_taps(n, kb_ref, other_ref)
    blank = jnp.zeros((128, 128), BF)
    for at, t in enumerate(REACH[0][0] + REACH[0][1] + REACH[1][0] + REACH[1][1]):
        taps = [tap(3 * t + c).astype(F32) for c in range(3)]
        both = jnp.concatenate([taps[1], taps[2]], axis=0).T.astype(BF)
        low = jnp.concatenate([jnp.zeros((64, 128), F32), taps[0]], axis=0).T.astype(BF)
        for r, (left, right) in enumerate(((both, blank), (low, both), (blank, low))):
            row = 384 * at + 128 * r
            tb_ref[row : row + 128, 0:128] = left
            tb_ref[row : row + 128, 128:256] = right


def grad_a_kernel(n, kb_ref, other_ref, h_ref, h0_ref, c_ref, vd_ref, vdh_ref, keep_ref, send_ref, tb_ref, d_ref, both_ref):
    slab = 16 // n
    planes = 2 * slab
    build_transposed(n, kb_ref, other_ref, tb_ref)
    read = hidden_reader(h_ref, h0_ref)
    row = 0
    for par in range(2):
        for hp in range(2):
            parts = []
            for t in REACH[par][hp]:
                up = 1 if t < 3 else 0
                slot = 1 if t % 3 == 0 else 0
                parts.append(jnp.concatenate([c_ref[p + up, slot, 0:128, :] for p in range(slab)], axis=0))
                parts.append(jnp.concatenate([c_ref[p + up, slot, 16:144, 0:128] for p in range(slab)], axis=0))
            size = 192 * len(parts)
            back = dot(jnp.concatenate(parts, axis=1), tb_ref[row : row + size, :])
            row += size
            back = back.astype(BF).astype(F32)
            for p in range(slab):
                u = 2 * p + par
                mask = read(u, 1 + hp, 16, 0, 256).astype(F32) > 0
                v = back[128 * p : 128 * p + 128]
                v = jnp.where(mask, v, 0.3 * v).T
                at = 512 * u + 256 * hp
                d_ref[0:128, at : at + 128] = v[0:128].astype(BF)
                d_ref[128:192, at : at + 128] = v[128:192].astype(BF)
                d_ref[0:128, at + 128 : at + 256] = v[128:256].astype(BF)
                d_ref[128:192, at + 128 : at + 256] = next_group(v[0:64]).astype(BF)
    left = iota((64, 128), 1) < 32
    pieces = []
    for first in range(0, 9, 2):
        columns = []
        for t in range(first, min(first + 2, 9)):
            a, b = t // 3, t % 3
            tiles = []
            for u in range(planes):
                src = sub(vdh_ref) if 2 * u + a == 0 else sub(vd_ref, 2 * u + a - 1)
                tiles += [src(2 * hp + b, 16, 128 * k, 128) for hp in range(2) for k in range(2)]
            columns.append(jnp.concatenate(tiles, axis=0))
        both = dot(d_ref[...], jnp.concatenate(columns, axis=1))
        for j in range(len(columns)):
            g = both[:, 128 * j : 128 * j + 128]
            pieces.append(
                jnp.where(left, pltpu.roll(g[128:192], 32, 1), pltpu.roll(g[0:64], 32, 1))
                + pltpu.roll(g[64:128], 96, 1)
            )
    pieces.append(jnp.zeros((64, 128), F32))
    for k in range(PAIRS):
        both = jnp.concatenate([pieces[2 * k], pieces[2 * k + 1]], axis=0).T
        for j in range(6):
            put_half(both_ref, 6 * k + j, both[16 * j : 16 * j + 16])
    split_halves(6 * PAIRS, both_ref, keep_ref, send_ref)


def features_kernel(n, kb_ref, other_ref, h_ref, h0_ref, *refs):
    outs, (piece_ref, tb_ref) = refs[:n], refs[n:]
    slab = 16 // n
    lanes = n
    build_second(n, kb_ref, other_ref, tb_ref)
    read = hidden_reader(h_ref, h0_ref)
    terms = [dot(second_rows(read, a, slab), tb_ref[1152 * a : 1152 * a + 1152, :]) for a in range(3)]
    local = terms[1] + terms[2]
    total = jnp.concatenate(
        [local[0:128], local[128:] + terms[0][: 128 * slab - 128], terms[0][128 * slab - 128 :]], axis=0
    ).astype(BF)
    wide = []
    for p in range(slab + 1):
        for m in range(16 // lanes):
            at = 128 * p + 16 * (m * lanes // 2)
            wide.append(
                jnp.concatenate([total[at + 16 * k : at + 16 * k + 16] for k in range(lanes // 2)], axis=1)
            )
    packed = dot(jnp.concatenate(wide, axis=0), lane_order(n, True)).astype(BF)
    for z in range(n):
        piece_ref[z] = packed[:, 128 * z : 128 * z + 128]
    me = lax.axis_index("mp")
    for d in range(n):
        outs[d][...] = piece_ref[(me + d) % n]


def pair_kernel(mine_b, got_b, keep_a, got_a, out_ref):
    core = core_of()
    out_ref[:, 0:64, :] = (mine_b[core] + got_b[core]).astype(BF)
    out_ref[:, 64:80, :] = (keep_a[...] + got_a[...]).astype(BF)


def sum_kernel(n, scale_a, scale_b, in_ref, out_ref):
    chan = 64 // n
    total = in_ref[0].astype(F32)
    for k in range(1, in_ref.shape[0]):
        total = total + in_ref[k].astype(F32)
    tap = total[0:64] * scale_b
    rest = total[64:80] * scale_a
    for g in range(out_ref.shape[0]):
        z = order(n)[g % n]
        out_ref[g, 0:chan, :] = tap[z * chan : z * chan + chan].astype(BF)
        out_ref[g, chan : chan + 16, :] = rest.astype(BF)


def unpack_kernel(n, *refs):
    ins, out_ref = refs[:n], refs[n]
    chan = out_ref.shape[4]
    lanes = 128 // chan
    rows = 256 // lanes
    per = 16 // n
    row = iota((256, 256), 0)
    col = iota((256, 256), 1)
    source = (col % 16) * 16 + ((col % rows) // 16) * lanes + col // rows
    pick = (row == source).astype(F32).astype(BF)
    me = lax.axis_index("mp")
    for d in range(n):
        first = (me + n - d) % n * per
        for p in range(per):
            z = ins[d][p * rows : p * rows + rows, :].astype(F32)
            if p == 0:
                more = ins[(d + 1) % n][per * rows : per * rows + rows, :].astype(F32)
                z = z + jnp.where(first > 0, more, 0.0)
            x = jnp.concatenate([z[:, chan * l : chan * l + chan] for l in range(lanes)], axis=0).astype(BF)
            out_ref[0, first + p] = dot(pick, x).astype(BF).reshape(16, 16, chan)


def last_kernel(mine_ref, other_ref, a_ref, b_ref):
    chan = b_ref.shape[1]
    first = core_of() == 0
    for j in range(15):
        x, y = mine_ref[j].astype(F32), other_ref[j].astype(F32)
        x, y = jnp.where(first, x, y), jnp.where(first, y, x)
        if 2 * j < TAPS:
            b_ref[2 * j] = x[0:chan]
        if 2 * j + 1 < TAPS:
            b_ref[2 * j + 1] = y[0:chan]
        v = jnp.concatenate([x[chan : chan + 16], y[chan : chan + 16]], axis=0)
        for half in range(2):
            t = 2 * (j // 3) + half
            if t < 9:
                a_ref[t // 3, t % 3, j % 3] = v[:, 64 * half : 64 * half + 64]


def call(body, outs, ins, us, scratch=(), mib=16):
    return pl.pallas_call(
        body,
        out_shape=outs,
        grid=(1,),
        in_specs=[VMEM] * ins if isinstance(ins, int) else ins,
        out_specs=[VMEM] * len(outs) if isinstance(outs, (list, tuple)) else VMEM,
        scratch_shapes=list(scratch),
        compiler_params=params(mib),
        cost_estimate=cost(us),
    )


def shards(volume, kernel_a, kernel_b, cotangent):
    n = lax.axis_size("mp")
    dp = lax.axis_size("dp")
    planes = volume.shape[1]
    hplanes = planes // 2
    slab = hplanes // 2
    chan_b = kernel_b.shape[3]
    chan_o = cotangent.shape[4]
    rows = 256 // (128 // chan_o)
    shape = jax.ShapeDtypeStruct
    up = [(i, i + 1) for i in range(n - 1)]
    swap = [(i, i ^ 1) for i in range(dp)]
    groups = [[(2 * k + c) * n + z for k in range(dp // 2) for z in order(n)] for c in range(2)]
    peers = dp * n // 2

    def exchange(x):
        return lax.all_to_all(x, ("dp", "mp"), 0, 0, tiled=True, axis_index_groups=groups)

    volume, cotangent, kernel_b = (
        pltpu.with_memory_space_constraint(x, pltpu.HBM) for x in (volume, cotangent, kernel_b.reshape(TAPS, chan_b, 128))
    )
    sent = (slab + 1) * rows + HALF * chan_b
    halo = pl.pallas_call(
        plane_kernel,
        out_shape=pltpu.VMEM((64, 2048), BF),
        in_specs=[pl.BlockSpec(memory_space=pltpu.HBM)],
        out_specs=VMEM,
        scratch_shapes=[pltpu.SemaphoreType.DMA],
        compiler_params=params(2),
        cost_estimate=cost(1),
    )(volume)
    packed = pl.pallas_call(
        functools.partial(pack_kernel, n),
        grid=(1,),
        out_shape=shape((n, sent, 128), BF),
        in_specs=[
            pl.BlockSpec(cotangent.shape, lambda i: (0, 0, 0, 0, 0)),
            pl.BlockSpec((TAPS, chan_b, 128), lambda i: (0, 0, 0)),
            pl.BlockSpec(memory_space=pl.ANY),
        ],
        out_specs=pl.BlockSpec((n, sent, 128), lambda i: (0, 0, 0)),
        compiler_params=params(8),
        cost_estimate=cost(2),
    )(cotangent, kernel_b, halo)
    halo = lax.ppermute(halo, "mp", up)
    cot = lax.all_to_all(packed, "mp", 0, 0, tiled=True, axis_index_groups=[order(n)])
    vd, hidden, pre = pl.pallas_call(
        first_kernel,
        out_shape=(
            pltpu.HBM((planes, 5, 144, 256), BF),
            pltpu.VMEM((hplanes, 3, 144, 256), BF),
            pltpu.VMEM((256, 256), F32),
        ),
        in_specs=[pl.BlockSpec(memory_space=pltpu.HBM), VMEM],
        out_specs=(pl.BlockSpec(memory_space=pltpu.HBM), VMEM, VMEM),
        scratch_shapes=[
            pltpu.VMEM((planes // 4, 4, 64, 2048), BF),
            pltpu.VMEM((planes + 1, 5, 144, 256), BF),
            pltpu.VMEM((3456, 256), BF),
            pltpu.SemaphoreType.DMA((planes // 4,)),
            pltpu.SemaphoreType.DMA((planes // 4,)),
        ],
        compiler_params=params(24),
        cost_estimate=cost(100),
    )(volume, kernel_a)
    hbm = pl.BlockSpec(memory_space=pltpu.HBM)
    vdh, h0 = pl.pallas_call(
        halo_kernel,
        out_shape=(pltpu.HBM((5, 144, 256), BF), pltpu.VMEM((3, 144, 256), BF)),
        in_specs=[VMEM, VMEM, VMEM],
        out_specs=(hbm, VMEM),
        scratch_shapes=[
            pltpu.VMEM((5, 144, 256), BF),
            pltpu.VMEM((1152, 256), BF),
            pltpu.SemaphoreType.DMA,
        ],
        compiler_params=params(16),
        cost_estimate=cost(10),
    )(halo, kernel_a, pre)
    cot, h0 = lax.optimization_barrier((cot, h0))
    kb_other = lax.ppermute(cot, "dp", swap)

    c, mine_b = call(
        functools.partial(grad_b_kernel, n),
        (pltpu.VMEM((slab + 1, 2, 144, 256), BF), pltpu.VMEM((2, peers, 64, 128), F32)),
        3,
        3,
    )(hidden, h0, cot)
    got_b = lax.ppermute(mine_b, "dp", swap)

    keep_a, send_a = call(
        functools.partial(grad_a_kernel, n),
        (shape((peers, 16, 128), F32), shape((peers, 16, 128), F32)),
        7,
        8,
        [pltpu.VMEM((3456, 256), BF), pltpu.VMEM((192, hplanes * 512), BF), pltpu.VMEM((2, peers, 16, 128), F32)],
        24,
    )(cot, kb_other, hidden, h0, c, vd, vdh)
    got_a = lax.ppermute(send_a, "dp", swap)

    sums = call(pair_kernel, pltpu.VMEM((peers, 80, 128), BF), 4, 1)(mine_b, got_b, keep_a, got_a)
    sums = exchange(sums)

    pieces = call(
        functools.partial(features_kernel, n),
        [shape(((slab + 1) * rows, 128), BF)] * n,
        4,
        4,
        [
            pltpu.VMEM((n, (slab + 1) * rows, 128), BF),
            pltpu.VMEM((3456, 256), BF),
        ],
    )(cot, kb_other, hidden, h0)
    pieces = list(pieces)
    early = (1,)

    def send(d):
        pieces[d] = lax.ppermute(pieces[d], "mp", [(i, (i + d) % n) for i in range(n)])

    for d in early:
        send(d)
    sums, *pieces = lax.optimization_barrier((sums, *pieces))
    for d in range(1, n):
        if d not in early:
            send(d)

    samples = volume.shape[0] * dp
    scale_a = 1 / math.sqrt(samples * (GRID // 2) ** 3)
    scale_b = 1 / math.sqrt(samples * (GRID // 4) ** 3)
    mine = call(
        functools.partial(sum_kernel, n, scale_a, scale_b), pltpu.VMEM((peers, chan_b + 16, 128), BF), 1, 1
    )(sums)
    mine = exchange(mine)
    mine, *pieces = lax.optimization_barrier((mine, *pieces))
    other = lax.ppermute(mine, "dp", swap)

    features = call(functools.partial(unpack_kernel, n), shape((1, 16, 16, 16, chan_o), BF), n, 2)(*pieces)
    grad_a, grad_b = call(
        last_kernel, (shape((3, 3, 3, 32, 64), F32), shape((TAPS, chan_b, 128), F32)), 2, 1
    )(mine, other)
    return (features, grad_a, grad_b.reshape(3, 3, 3, chan_b, 128))


def solution(mesh):
    return jax.shard_map(
        shards,
        mesh=mesh,
        in_specs=(
            P("dp", "mp", None, None),
            P(),
            P(None, None, None, "mp", None),
            P("dp", None, None, None, "mp"),
        ),
        out_specs=(P("dp", None, None, None, "mp"), P(), P(None, None, None, "mp", None)),
        check_vma=False,
    )
```

```python
import functools
import math

import jax
import jax.numpy as jnp
from jax import lax
from jax.experimental import pallas as pl
from jax.experimental.pallas import tpu as pltpu
from jax.sharding import PartitionSpec as P

GRID = 64
BF = jnp.bfloat16
F32 = jnp.float32
VMEM = pl.BlockSpec(memory_space=pltpu.VMEM)
TAPS = 27
HALF = 14
PAIRS = 5
MIB = 1 << 20


def dot(a, b):
    return lax.dot_general(a, b, (((1,), (0,)), ((), ())), preferred_element_type=F32)


def iota(shape, dim):
    return lax.broadcasted_iota(jnp.int32, shape, dim)


def params(mib):
    return pltpu.CompilerParams(vmem_limit_bytes=mib * MIB)


def cost(us):
    return pl.CostEstimate(flops=int(us * 1e9), bytes_accessed=int(us * 3e6), transcendentals=0)


def deinterleave(x, count):
    row = iota((80 * count, 64 * count), 0)
    col = iota((80 * count, 64 * count), 1)
    h = 4 * (row % 16) + row % 80 // 16 - 1
    pick = jnp.logical_and(h >= 0, col == row // 80 * 64 + h).astype(F32).astype(BF)
    return dot(pick, x).astype(BF)


def store_plane(ref, lead, y, row):
    for slot in range(5):
        ref[(*lead, slot, slice(0, 16))] = jnp.zeros((16, 256), BF)
        for s in range(8):
            at = row + 16 * slot
            ref[(*lead, slot, slice(16 + 16 * s, 32 + 16 * s))] = y[at : at + 16, 256 * s : 256 * s + 256]


def build_first(ka_ref, ta_ref, taps=9):
    left = iota((32, 128), 1) < 64
    zero = jnp.zeros((32, 128), F32)
    for t in range(taps):
        wide = []
        for c in range(3):
            k = ka_ref[t // 3, t % 3, c].astype(F32)
            wide.append(jnp.concatenate([k, k], axis=1))
        for half in range(2):
            for w in range(-4, 8):
                row = 384 * t + (32 * w if w >= 0 else 256 + 32 * (w + 4))
                c0 = w - 4 * half + 1
                c1 = c0 - 2
                l = wide[c0] if 0 <= c0 <= 2 else zero
                r = wide[c1] if 0 <= c1 <= 2 else zero
                ta_ref[row : row + 32, 128 * half : 128 * half + 128] = jnp.where(left, l, r).astype(BF)


def first_rows(plane, b):
    main = jnp.concatenate([plane(b, 16, 0, 256), plane(b + 2, 16, 0, 256)], axis=0)
    edge = jnp.concatenate([plane(b, 0, 128, 128), plane(b + 2, 0, 128, 128)], axis=0)
    return [main, edge]


def first_term(planes, a, ta_ref):
    parts = []
    for b in range(3):
        both = [first_rows(plane, b) for plane in planes]
        parts.append(jnp.concatenate([m for m, _ in both], axis=0))
        parts.append(jnp.concatenate([e for _, e in both], axis=0))
    return dot(jnp.concatenate(parts, axis=1), ta_ref[1152 * a : 1152 * a + 1152, :])


def down_shift(x):
    moved = pltpu.roll(x, 1, 0)
    return jnp.where(iota(x.shape, 0) % 16 == 0, 0.0, moved)


def next_group(x):
    moved = pltpu.roll(x, 112, 1)
    return jnp.where(iota(x.shape, 1) >= 112, 0.0, moved)


def up_shift(x):
    moved = pltpu.roll(x, x.shape[0] - 1, 0)
    return jnp.where(iota(x.shape, 0) % 16 == 15, 0.0, moved)


def store_hidden(put, even, odd):
    put(0, down_shift(odd).astype(BF))
    put(1, even.astype(BF))
    put(2, odd.astype(BF))


def leaky(pre):
    return jnp.where(pre > 0, pre, 0.3 * pre)


def sub(ref, *lead):
    def read(slot, row, lane, width):
        return ref[(*lead, slot, slice(row, row + 128), slice(lane, lane + width))]

    return read


def first_kernel(vol_ref, ka_ref, out_ref, h_ref, pre_ref, x_ref, vd_ref, ta_ref, sems, out_sems):
    steps = x_ref.shape[0]

    def fetch(i):
        return pltpu.make_async_copy(vol_ref.at[0, pl.ds(4 * i, 4)], x_ref.at[i], sems.at[i])

    def flush(i):
        return pltpu.make_async_copy(
            vd_ref.at[pl.ds(4 * i + 1, 4)], out_ref.at[pl.ds(4 * i, 4)], out_sems.at[i]
        )

    for i in range(steps):
        fetch(i).start()
    build_first(ka_ref, ta_ref)
    vd_ref[0] = jnp.zeros((5, 144, 256), BF)

    @pl.loop(0, steps)
    def _(i):
        fetch(i).wait()
        y = deinterleave(x_ref[i].reshape(256, 2048), 4)
        for k in range(4):
            store_plane(vd_ref, (4 * i + k + 1,), y, 80 * k)
        flush(i).start()
        total = None
        for a in range(3):
            term = first_term([sub(vd_ref, 4 * i + a), sub(vd_ref, 4 * i + a + 2)], a, ta_ref)
            total = term if total is None else total + term

        @pl.when(i == 0)
        def _():
            pre_ref[...] = total[0:256]

        hid = leaky(total)
        for k in range(2):

            def put(slot, x):
                h_ref[2 * i + k, slot, 0:16, :] = jnp.zeros((16, 256), BF)
                h_ref[2 * i + k, slot, 16:144, :] = x

            store_hidden(put, hid[256 * k : 256 * k + 128], hid[256 * k + 128 : 256 * k + 256])

    for i in range(steps):
        flush(i).wait()


def core_of():
    return lax.axis_index("dp") % 2


def plane_kernel(vol_ref, out_ref, sem):
    copy = pltpu.make_async_copy(vol_ref.at[0, vol_ref.shape[1] - 1], out_ref, sem)
    copy.start()
    copy.wait()


def pack_kernel(n, cot_ref, kb_ref, after_ref, *refs):
    del after_ref
    outs, full_ref = refs[:n], refs[n]
    chan = cot_ref.shape[4]
    lanes = 128 // chan
    rows = 256 // lanes
    per = 16 // n
    row = iota((256, 256), 0)
    col = iota((256, 256), 1)
    source = (row % 16) * 16 + ((row % rows) // 16) * lanes + row // rows
    pick = (col == source).astype(F32).astype(BF)
    for p in range(16):
        y = dot(pick, cot_ref[0, p].reshape(256, chan))
        z = jnp.concatenate([y[rows * l : rows * l + rows] for l in range(lanes)], axis=1).astype(BF)
        t = p // per
        at = (p % per) * rows
        full_ref[t, at : at + rows, :] = z
        if p % per == 0 and t > 0:
            full_ref[t - 1, per * rows : per * rows + rows, :] = z
    full_ref[n - 1, per * rows : per * rows + rows, :] = jnp.zeros((rows, 128), BF)
    me = lax.axis_index("mp")
    first = 13 * core_of()
    size = kb_ref.shape[1]
    head = (per + 1) * rows
    for d in range(n):
        outs[d][0:head, :] = full_ref[(me + d) % n]
        for j in range(HALF):
            outs[d][head + size * j : head + size * j + size, :] = kb_ref[first + j]


def gather_kernel(n, *refs):
    pieces, (cot_ref, kb_ref) = refs[:n], refs[n:]
    head, tail = cot_ref.shape[1], kb_ref.shape[1]
    me = lax.axis_index("mp")
    for d in range(n):
        cot_ref[(me + n - d) % n] = pieces[d][0:head, :]
        kb_ref[(me + n - d) % n] = pieces[d][head : head + tail, :]


def lane_order(n, inverse):
    size = n * 128
    chan = 128 // n
    row = iota((size, size), 0)
    col = iota((size, size), 1)
    if inverse:
        row, col = col, row
    target = ((row // chan) % n) * 128 + (row // 128) * chan + row % chan
    return (col == target).astype(F32).astype(BF)


def slab_planes(a, count):
    return [2 * p + a - 1 for p in range(count + 1)][1 if a == 0 else 0 :][:count]


def second_rows(hread, a, count):
    planes = slab_planes(a, count)
    parts = []
    for b in range(3):
        parts.append(jnp.concatenate([hread(u, b, 16, 0, 256) for u in planes], axis=0))
        parts.append(jnp.concatenate([hread(u, b, 0, 128, 128) for u in planes], axis=0))
    return jnp.concatenate(parts, axis=1)


def hidden_reader(h_ref, h0_ref):
    def read(index, slot, row, lane, width):
        rows, cols = slice(row, row + 128), slice(lane, lane + width)
        return h0_ref[slot, rows, cols] if index == 0 else h_ref[index, slot, rows, cols]

    return read


def put_in(ref):
    def put(slot, v):
        ref[slot, 0:16, :] = jnp.zeros((16, 256), BF)
        ref[slot, 16:144, :] = v

    return put


def put_half(both_ref, item, v):
    both_ref[(item + core_of()) % 2, item // 2] = v


def split_halves(count, both_ref, keep_ref, send_ref):
    zero = jnp.zeros(keep_ref.shape[1:], F32)
    for item in range(count, 2 * keep_ref.shape[0]):
        put_half(both_ref, item, zero)
    keep_ref[...] = both_ref[0]
    send_ref[...] = both_ref[1]


def halo_kernel(halo_ref, ka_ref, pre_ref, vd_out, h0_ref, vdh_ref, ta_ref, sem):
    build_first(ka_ref, ta_ref, 3)
    store_plane(vdh_ref, (), deinterleave(halo_ref[...], 1), 0)
    flush = pltpu.make_async_copy(vdh_ref, vd_out, sem)
    flush.start()
    hid = leaky(pre_ref[...] + first_term([sub(vdh_ref)], 0, ta_ref))
    store_hidden(put_in(h0_ref), hid[0:128], hid[128:256])
    flush.wait()


def grad_b_kernel(n, h_ref, h0_ref, cot_ref, c_ref, both_ref):
    slab = 16 // n
    lanes = n
    rows = 256 // lanes
    wide = jnp.concatenate([cot_ref[t] for t in range(n)], axis=1)
    turned = dot(wide, lane_order(n, False))
    turns = []
    for p in range(slab + 1):
        main = jnp.concatenate(
            [
                turned[
                    p * rows + 16 * (2 * s // lanes) : p * rows + 16 * (2 * s // lanes) + 16,
                    128 * (2 * s % lanes) : 128 * (2 * s % lanes) + 256,
                ]
                for s in range(8)
            ],
            axis=0,
        )
        turn = main.T
        one = jnp.concatenate([turn[0:128], turn[128:256]], axis=1)
        two = jnp.concatenate([turn[128:256], next_group(turn[0:128])], axis=1)
        turns.append(jnp.concatenate([one, two], axis=0).astype(BF))
        for slot, v in enumerate((main, up_shift(main))):
            c_ref[p, slot, 0:128, :] = v.astype(BF)
            c_ref[p, slot, 128:144, :] = jnp.zeros((16, 256), BF)
    read = hidden_reader(h_ref, h0_ref)
    for a in range(3):
        first = 1 if a == 0 else 0
        turn = jnp.concatenate(turns[first : first + slab], axis=1)
        columns = []
        for b in range(3):
            tiles = [read(u, b, 16, 128 * k, 128) for u in slab_planes(a, slab) for k in range(2)]
            columns.append(jnp.concatenate(tiles, axis=0))
        g = dot(turn, jnp.concatenate(columns, axis=1))
        for b in range(3):
            t = 3 * a + b
            one = g[0:128, 128 * b : 128 * b + 128].T
            two = g[128:256, 128 * b : 128 * b + 128].T
            both_ref[3 * t % 2, 3 * t // 2] = two[64:128]
            both_ref[(3 * t + 1) % 2, (3 * t + 1) // 2] = one[0:64]
            both_ref[(3 * t + 2) % 2, (3 * t + 2) // 2] = one[64:128]
    for item in range(TAPS, 2 * both_ref.shape[1]):
        both_ref[item % 2, item // 2] = jnp.zeros(both_ref.shape[2:], F32)


def second_taps(n, kb_ref, other_ref):
    chan = 64 // n
    first = core_of() == 0

    def tap(k):
        j, own_first = (k, True) if k < 13 else (k - 13, False)
        parts = []
        for z in range(n):
            own = kb_ref[z, j * chan : j * chan + chan, :]
            other = other_ref[z, j * chan : j * chan + chan, :]
            pair = (own, other) if own_first else (other, own)
            parts.append(jnp.where(first, *pair))
        return jnp.concatenate(parts, axis=0)

    return tap


def build_second(n, kb_ref, other_ref, tb_ref):
    tap = second_taps(n, kb_ref, other_ref)
    blank = jnp.zeros((64, 128), BF)
    for t in range(9):
        taps = [tap(3 * t + c) for c in range(3)]
        for w in range(-2, 4):
            row = 384 * t + (64 * w if w >= 0 else 256 + 64 * (w + 2))
            for r in range(2):
                c = w - 2 * r + 1
                tb_ref[row : row + 64, 128 * r : 128 * r + 128] = taps[c] if 0 <= c <= 2 else blank


REACH = (((4,), (3, 5)), ((1, 7), (0, 2, 6, 8)))


def build_transposed(n, kb_ref, other_ref, tb_ref):
    tap = second_taps(n, kb_ref, other_ref)
    blank = jnp.zeros((128, 128), BF)
    for at, t in enumerate(REACH[0][0] + REACH[0][1] + REACH[1][0] + REACH[1][1]):
        taps = [tap(3 * t + c).astype(F32) for c in range(3)]
        both = jnp.concatenate([taps[1], taps[2]], axis=0).T.astype(BF)
        low = jnp.concatenate([jnp.zeros((64, 128), F32), taps[0]], axis=0).T.astype(BF)
        for r, (left, right) in enumerate(((both, blank), (low, both), (blank, low))):
            row = 384 * at + 128 * r
            tb_ref[row : row + 128, 0:128] = left
            tb_ref[row : row + 128, 128:256] = right


def grad_a_kernel(n, kb_ref, other_ref, h_ref, h0_ref, c_ref, vd_ref, vdh_ref, keep_ref, send_ref, tb_ref, d_ref, both_ref):
    slab = 16 // n
    planes = 2 * slab
    build_transposed(n, kb_ref, other_ref, tb_ref)
    read = hidden_reader(h_ref, h0_ref)
    row = 0
    for par in range(2):
        for hp in range(2):
            parts = []
            for t in REACH[par][hp]:
                up = 1 if t < 3 else 0
                slot = 1 if t % 3 == 0 else 0
                parts.append(jnp.concatenate([c_ref[p + up, slot, 0:128, :] for p in range(slab)], axis=0))
                parts.append(jnp.concatenate([c_ref[p + up, slot, 16:144, 0:128] for p in range(slab)], axis=0))
            size = 192 * len(parts)
            back = dot(jnp.concatenate(parts, axis=1), tb_ref[row : row + size, :])
            row += size
            back = back.astype(BF).astype(F32)
            for p in range(slab):
                u = 2 * p + par
                mask = read(u, 1 + hp, 16, 0, 256).astype(F32) > 0
                v = back[128 * p : 128 * p + 128]
                v = jnp.where(mask, v, 0.3 * v).T
                at = 512 * u + 256 * hp
                d_ref[0:128, at : at + 128] = v[0:128].astype(BF)
                d_ref[128:192, at : at + 128] = v[128:192].astype(BF)
                d_ref[0:128, at + 128 : at + 256] = v[128:256].astype(BF)
                d_ref[128:192, at + 128 : at + 256] = next_group(v[0:64]).astype(BF)
    left = iota((64, 128), 1) < 32
    pieces = []
    for first in range(0, 9, 2):
        columns = []
        for t in range(first, min(first + 2, 9)):
            a, b = t // 3, t % 3
            tiles = []
            for u in range(planes):
                src = sub(vdh_ref) if 2 * u + a == 0 else sub(vd_ref, 2 * u + a - 1)
                tiles += [src(2 * hp + b, 16, 128 * k, 128) for hp in range(2) for k in range(2)]
            columns.append(jnp.concatenate(tiles, axis=0))
        both = dot(d_ref[...], jnp.concatenate(columns, axis=1))
        for j in range(len(columns)):
            g = both[:, 128 * j : 128 * j + 128]
            pieces.append(
                jnp.where(left, pltpu.roll(g[128:192], 32, 1), pltpu.roll(g[0:64], 32, 1))
                + pltpu.roll(g[64:128], 96, 1)
            )
    pieces.append(jnp.zeros((64, 128), F32))
    for k in range(PAIRS):
        both = jnp.concatenate([pieces[2 * k], pieces[2 * k + 1]], axis=0).T
        for j in range(6):
            put_half(both_ref, 6 * k + j, both[16 * j : 16 * j + 16])
    split_halves(6 * PAIRS, both_ref, keep_ref, send_ref)


def features_kernel(n, kb_ref, other_ref, h_ref, h0_ref, *refs):
    outs, (piece_ref, tb_ref) = refs[:n], refs[n:]
    slab = 16 // n
    lanes = n
    build_second(n, kb_ref, other_ref, tb_ref)
    read = hidden_reader(h_ref, h0_ref)
    terms = [dot(second_rows(read, a, slab), tb_ref[1152 * a : 1152 * a + 1152, :]) for a in range(3)]
    local = terms[1] + terms[2]
    total = jnp.concatenate(
        [local[0:128], local[128:] + terms[0][: 128 * slab - 128], terms[0][128 * slab - 128 :]], axis=0
    ).astype(BF)
    wide = []
    for p in range(slab + 1):
        for m in range(16 // lanes):
            at = 128 * p + 16 * (m * lanes // 2)
            wide.append(
                jnp.concatenate([total[at + 16 * k : at + 16 * k + 16] for k in range(lanes // 2)], axis=1)
            )
    packed = dot(jnp.concatenate(wide, axis=0), lane_order(n, True)).astype(BF)
    for z in range(n):
        piece_ref[z] = packed[:, 128 * z : 128 * z + 128]
    me = lax.axis_index("mp")
    for d in range(n):
        outs[d][...] = piece_ref[(me + d) % n]


def per_column(columns):
    return -(-14 // columns), -(-15 // columns)


def pair_kernel(columns, mine_b, got_b, keep_a, got_a, *outs):
    taps, chunks = per_column(columns)
    core = core_of()
    k = lax.axis_index("dp") // 2
    for m in range(columns):
        to = jnp.bitwise_xor(k, m)
        for s in range(taps):
            j = to * taps + s
            outs[m][64 * s : 64 * s + 64, :] = (mine_b[core, j] + got_b[core, j]).astype(BF)
        for s in range(chunks):
            j = to * chunks + s
            at = 64 * taps + 16 * s
            outs[m][at : at + 16, :] = (keep_a[j] + got_a[j]).astype(BF)


def column_sum_kernel(n, columns, *refs):
    ins, outs, piece_ref = refs[:columns], refs[columns : columns + n], refs[columns + n]
    taps, chunks = per_column(columns)
    chan = 64 // n
    total = ins[0][...].astype(F32)
    for m in range(1, columns):
        total = total + ins[m][...].astype(F32)
    total = total.astype(BF)
    for z in range(n):
        for s in range(taps):
            at = 64 * s + chan * z
            piece_ref[z, chan * s : chan * s + chan, :] = total[at : at + chan]
        piece_ref[z, chan * taps :, :] = total[64 * taps :]
    me = lax.axis_index("mp")
    for d in range(n):
        outs[d][...] = piece_ref[(me + d) % n]


def slab_sum_kernel(n, columns, scale_a, scale_b, *refs):
    ins, out_ref = refs[:n], refs[n]
    split = 64 // n * per_column(columns)[0]
    total = ins[0][...].astype(F32)
    for d in range(1, n):
        total = total + ins[d][...].astype(F32)
    out_ref[0:split, :] = (total[0:split] * scale_b).astype(BF)
    out_ref[split:, :] = (total[split:] * scale_a).astype(BF)


def unpack_kernel(n, *refs):
    ins, out_ref = refs[:n], refs[n]
    chan = out_ref.shape[4]
    lanes = 128 // chan
    rows = 256 // lanes
    per = 16 // n
    row = iota((256, 256), 0)
    col = iota((256, 256), 1)
    source = (col % 16) * 16 + ((col % rows) // 16) * lanes + col // rows
    pick = (row == source).astype(F32).astype(BF)
    me = lax.axis_index("mp")
    for d in range(n):
        first = (me + n - d) % n * per
        for p in range(per):
            z = ins[d][p * rows : p * rows + rows, :].astype(F32)
            if p == 0:
                more = ins[(d + 1) % n][per * rows : per * rows + rows, :].astype(F32)
                z = z + jnp.where(first > 0, more, 0.0)
            x = jnp.concatenate([z[:, chan * l : chan * l + chan] for l in range(lanes)], axis=0).astype(BF)
            out_ref[0, first + p] = dot(pick, x).astype(BF).reshape(16, 16, chan)


def last_kernel(columns, *refs):
    mine, other, (a_ref, b_ref, chunk_ref, tap_ref) = refs[:columns], refs[columns : 2 * columns], refs[2 * columns :]
    taps, chunks = per_column(columns)
    chan = b_ref.shape[1]
    core = core_of()
    k = lax.axis_index("dp") // 2
    for m in range(columns):
        owner = jnp.bitwise_xor(k, m)
        for piece, c in ((mine[m], core), (other[m], 1 - core)):
            for s in range(taps):
                tap_ref[2 * (owner * taps + s) + c] = piece[chan * s : chan * s + chan, :].astype(F32)
            for s in range(chunks):
                at = chan * taps + 16 * s
                chunk_ref[2 * (owner * chunks + s) + c] = piece[at : at + 16, :].astype(F32)
    b_ref[...] = tap_ref[0:TAPS]
    for j in range(15):
        v = jnp.concatenate([chunk_ref[2 * j], chunk_ref[2 * j + 1]], axis=0)
        for half in range(2):
            t = 2 * (j // 3) + half
            if t < 9:
                a_ref[t // 3, t % 3, j % 3] = v[:, 64 * half : 64 * half + 64]


def call(body, outs, ins, us, scratch=(), mib=16):
    return pl.pallas_call(
        body,
        out_shape=outs,
        grid=(1,),
        in_specs=[VMEM] * ins if isinstance(ins, int) else ins,
        out_specs=[VMEM] * len(outs) if isinstance(outs, (list, tuple)) else VMEM,
        scratch_shapes=list(scratch),
        compiler_params=params(mib),
        cost_estimate=cost(us),
    )


def shards(volume, kernel_a, kernel_b, cotangent):
    n = lax.axis_size("mp")
    dp = lax.axis_size("dp")
    planes = volume.shape[1]
    hplanes = planes // 2
    slab = hplanes // 2
    chan_b = kernel_b.shape[3]
    chan_o = cotangent.shape[4]
    rows = 256 // (128 // chan_o)
    shape = jax.ShapeDtypeStruct
    up = [(i, i + 1) for i in range(n - 1)]
    swap = [(i, i ^ 1) for i in range(dp)]
    columns = dp // 2
    taps, chunks = per_column(columns)

    def along_mp(x, d):
        return lax.ppermute(x, "mp", [(i, (i + d) % n) for i in range(n)])

    def along_dp(x, m):
        return lax.ppermute(x, "dp", [(i, i ^ (2 * m)) for i in range(dp)])

    volume, cotangent, kernel_b = (
        pltpu.with_memory_space_constraint(x, pltpu.HBM) for x in (volume, cotangent, kernel_b.reshape(TAPS, chan_b, 128))
    )
    sent = (slab + 1) * rows + HALF * chan_b
    halo = pl.pallas_call(
        plane_kernel,
        out_shape=pltpu.VMEM((64, 2048), BF),
        in_specs=[pl.BlockSpec(memory_space=pltpu.HBM)],
        out_specs=VMEM,
        scratch_shapes=[pltpu.SemaphoreType.DMA],
        compiler_params=params(2),
        cost_estimate=cost(1),
    )(volume)
    parts = list(
        pl.pallas_call(
            functools.partial(pack_kernel, n),
            grid=(1,),
            out_shape=[pltpu.VMEM((sent, 128), BF)] * n,
            in_specs=[
                pl.BlockSpec(cotangent.shape, lambda i: (0, 0, 0, 0, 0)),
                pl.BlockSpec((TAPS, chan_b, 128), lambda i: (0, 0, 0)),
                pl.BlockSpec(memory_space=pl.ANY),
            ],
            out_specs=[VMEM] * n,
            scratch_shapes=[pltpu.VMEM((n, (slab + 1) * rows, 128), BF)],
            compiler_params=params(8),
            cost_estimate=cost(2),
        )(cotangent, kernel_b, halo)
    )
    halo = lax.ppermute(halo, "mp", up)
    for d in range(1, n):
        parts[d] = lax.ppermute(parts[d], "mp", [(i, (i + d) % n) for i in range(n)])

    vd, hidden, pre = pl.pallas_call(
        first_kernel,
        out_shape=(
            pltpu.HBM((planes, 5, 144, 256), BF),
            pltpu.VMEM((hplanes, 3, 144, 256), BF),
            pltpu.VMEM((256, 256), F32),
        ),
        in_specs=[pl.BlockSpec(memory_space=pltpu.HBM), VMEM],
        out_specs=(pl.BlockSpec(memory_space=pltpu.HBM), VMEM, VMEM),
        scratch_shapes=[
            pltpu.VMEM((planes // 4, 4, 64, 2048), BF),
            pltpu.VMEM((planes + 1, 5, 144, 256), BF),
            pltpu.VMEM((3456, 256), BF),
            pltpu.SemaphoreType.DMA((planes // 4,)),
            pltpu.SemaphoreType.DMA((planes // 4,)),
        ],
        compiler_params=params(24),
        cost_estimate=cost(100),
    )(volume, kernel_a)
    hbm = pl.BlockSpec(memory_space=pltpu.HBM)
    vdh, h0 = pl.pallas_call(
        halo_kernel,
        out_shape=(pltpu.HBM((5, 144, 256), BF), pltpu.VMEM((3, 144, 256), BF)),
        in_specs=[VMEM, VMEM, VMEM],
        out_specs=(hbm, VMEM),
        scratch_shapes=[
            pltpu.VMEM((5, 144, 256), BF),
            pltpu.VMEM((1152, 256), BF),
            pltpu.SemaphoreType.DMA,
        ],
        compiler_params=params(16),
        cost_estimate=cost(10),
    )(halo, kernel_a, pre)
    h0, *parts = lax.optimization_barrier((h0, *parts))
    cot, kb = call(
        functools.partial(gather_kernel, n),
        (pltpu.VMEM((n, (slab + 1) * rows, 128), BF), pltpu.VMEM((n, HALF * chan_b, 128), BF)),
        n,
        1,
    )(*parts)
    kb_other = lax.ppermute(kb, "dp", swap)

    c, mine_b = call(
        functools.partial(grad_b_kernel, n),
        (pltpu.VMEM((slab + 1, 2, 144, 256), BF), pltpu.VMEM((2, columns * taps, 64, 128), F32)),
        3,
        3,
    )(hidden, h0, cot)
    got_b = lax.ppermute(mine_b, "dp", swap)

    keep_a, send_a = call(
        functools.partial(grad_a_kernel, n),
        (pltpu.VMEM((columns * chunks, 16, 128), F32), pltpu.VMEM((columns * chunks, 16, 128), F32)),
        7,
        8,
        [pltpu.VMEM((3456, 256), BF), pltpu.VMEM((192, hplanes * 512), BF), pltpu.VMEM((2, columns * chunks, 16, 128), F32)],
        24,
    )(kb, kb_other, hidden, h0, c, vd, vdh)
    got_a = lax.ppermute(send_a, "dp", swap)

    size = 64 * taps + 16 * chunks
    sums = list(
        call(functools.partial(pair_kernel, columns), [pltpu.VMEM((size, 128), BF)] * columns, 4, 1)(
            mine_b, got_b, keep_a, got_a
        )
    )
    for m in range(1, columns):
        sums[m] = along_dp(sums[m], m)
    pieces = list(
        call(
            functools.partial(features_kernel, n),
            [pltpu.VMEM(((slab + 1) * rows, 128), BF)] * n,
            4,
            4,
            [
                pltpu.VMEM((n, (slab + 1) * rows, 128), BF),
                pltpu.VMEM((3456, 256), BF),
            ],
        )(kb, kb_other, hidden, h0)
    )
    for d in range(1, n):
        pieces[d] = along_mp(pieces[d], d)

    size = chan_b * taps + 16 * chunks
    sums = list(
        call(
            functools.partial(column_sum_kernel, n, columns),
            [pltpu.VMEM((size, 128), BF)] * n,
            columns,
            1,
            [pltpu.VMEM((n, size, 128), BF)],
        )(*sums)
    )
    for d in range(1, n):
        sums[d] = along_mp(sums[d], d)
    both = lax.optimization_barrier((*sums, *pieces))
    sums, pieces = both[:n], both[n:]

    samples = volume.shape[0] * dp
    scale_a = 1 / math.sqrt(samples * (GRID // 2) ** 3)
    scale_b = 1 / math.sqrt(samples * (GRID // 4) ** 3)
    total = call(
        functools.partial(slab_sum_kernel, n, columns, scale_a, scale_b), pltpu.VMEM((size, 128), BF), n, 1
    )(*sums)
    mine = [total] + [along_dp(total, m) for m in range(1, columns)]
    features = call(functools.partial(unpack_kernel, n), shape((1, 16, 16, 16, chan_o), BF), n, 2)(*pieces)
    both = lax.optimization_barrier((features, *mine))
    features, mine = both[0], both[1:]
    other = [lax.ppermute(x, "dp", swap) for x in mine]
    grad_a, grad_b = call(
        functools.partial(last_kernel, columns),
        (shape((3, 3, 3, 32, 64), F32), shape((TAPS, chan_b, 128), F32)),
        2 * columns,
        1,
        [
            pltpu.VMEM((2 * columns * chunks, 16, 128), F32),
            pltpu.VMEM((2 * columns * taps, chan_b, 128), F32),
        ],
    )(*mine, *other)
    return (features, grad_a, grad_b.reshape(3, 3, 3, chan_b, 128))


def solution(mesh):
    return jax.shard_map(
        shards,
        mesh=mesh,
        in_specs=(
            P("dp", "mp", None, None),
            P(),
            P(None, None, None, "mp", None),
            P("dp", None, None, None, "mp"),
        ),
        out_specs=(P("dp", None, None, None, "mp"), P(), P(None, None, None, "mp", None)),
        check_vma=False,
    )
```

```python
import functools
import math

import jax
import jax.numpy as jnp
from jax import lax
from jax.experimental import pallas as pl
from jax.experimental.pallas import tpu as pltpu
from jax.sharding import PartitionSpec as P

GRID = 64
BF = jnp.bfloat16
F32 = jnp.float32
VMEM = pl.BlockSpec(memory_space=pltpu.VMEM)
TAPS = 27
HALF = 14
PAIRS = 5
MIB = 1 << 20


def dot(a, b):
    return lax.dot_general(a, b, (((1,), (0,)), ((), ())), preferred_element_type=F32)


def iota(shape, dim):
    return lax.broadcasted_iota(jnp.int32, shape, dim)


def params(mib):
    return pltpu.CompilerParams(vmem_limit_bytes=mib * MIB)


def cost(us):
    return pl.CostEstimate(flops=int(us * 1e9), bytes_accessed=int(us * 3e6), transcendentals=0)


def deinterleave(x, count):
    row = iota((80 * count, 64 * count), 0)
    col = iota((80 * count, 64 * count), 1)
    h = 4 * (row % 16) + row % 80 // 16 - 1
    pick = jnp.logical_and(h >= 0, col == row // 80 * 64 + h).astype(F32).astype(BF)
    return dot(pick, x).astype(BF)


def store_plane(ref, lead, y, row):
    for slot in range(5):
        ref[(*lead, slot, slice(0, 16))] = jnp.zeros((16, 256), BF)
        for s in range(8):
            at = row + 16 * slot
            ref[(*lead, slot, slice(16 + 16 * s, 32 + 16 * s))] = y[at : at + 16, 256 * s : 256 * s + 256]


def build_first(ka_ref, ta_ref, taps=9):
    left = iota((32, 128), 1) < 64
    zero = jnp.zeros((32, 128), F32)
    for t in range(taps):
        wide = []
        for c in range(3):
            k = ka_ref[t // 3, t % 3, c].astype(F32)
            wide.append(jnp.concatenate([k, k], axis=1))
        for half in range(2):
            for w in range(-4, 8):
                row = 384 * t + (32 * w if w >= 0 else 256 + 32 * (w + 4))
                c0 = w - 4 * half + 1
                c1 = c0 - 2
                l = wide[c0] if 0 <= c0 <= 2 else zero
                r = wide[c1] if 0 <= c1 <= 2 else zero
                ta_ref[row : row + 32, 128 * half : 128 * half + 128] = jnp.where(left, l, r).astype(BF)


def first_rows(plane, b):
    main = jnp.concatenate([plane(b, 16, 0, 256), plane(b + 2, 16, 0, 256)], axis=0)
    edge = jnp.concatenate([plane(b, 0, 128, 128), plane(b + 2, 0, 128, 128)], axis=0)
    return [main, edge]


def first_term(planes, a, ta_ref):
    parts = []
    for b in range(3):
        both = [first_rows(plane, b) for plane in planes]
        parts.append(jnp.concatenate([m for m, _ in both], axis=0))
        parts.append(jnp.concatenate([e for _, e in both], axis=0))
    return dot(jnp.concatenate(parts, axis=1), ta_ref[1152 * a : 1152 * a + 1152, :])


def down_shift(x):
    moved = pltpu.roll(x, 1, 0)
    return jnp.where(iota(x.shape, 0) % 16 == 0, 0.0, moved)


def next_group(x):
    moved = pltpu.roll(x, 112, 1)
    return jnp.where(iota(x.shape, 1) >= 112, 0.0, moved)


def up_shift(x):
    moved = pltpu.roll(x, x.shape[0] - 1, 0)
    return jnp.where(iota(x.shape, 0) % 16 == 15, 0.0, moved)


def store_hidden(put, even, odd):
    put(0, down_shift(odd).astype(BF))
    put(1, even.astype(BF))
    put(2, odd.astype(BF))


def leaky(pre):
    return jnp.where(pre > 0, pre, 0.3 * pre)


def sub(ref, *lead):
    def read(slot, row, lane, width):
        return ref[(*lead, slot, slice(row, row + 128), slice(lane, lane + width))]

    return read


def first_kernel(vol_ref, ka_ref, out_ref, h_ref, pre_ref, x_ref, vd_ref, ta_ref, sems, out_sems):
    steps = x_ref.shape[0]

    def fetch(i):
        return pltpu.make_async_copy(vol_ref.at[0, pl.ds(4 * i, 4)], x_ref.at[i], sems.at[i])

    def flush(i):
        return pltpu.make_async_copy(
            vd_ref.at[pl.ds(4 * i + 1, 4)], out_ref.at[pl.ds(4 * i, 4)], out_sems.at[i]
        )

    for i in range(steps):
        fetch(i).start()
    build_first(ka_ref, ta_ref)
    vd_ref[0] = jnp.zeros((5, 144, 256), BF)

    @pl.loop(0, steps)
    def _(i):
        fetch(i).wait()
        y = deinterleave(x_ref[i].reshape(256, 2048), 4)
        for k in range(4):
            store_plane(vd_ref, (4 * i + k + 1,), y, 80 * k)
        flush(i).start()
        total = None
        for a in range(3):
            term = first_term([sub(vd_ref, 4 * i + a), sub(vd_ref, 4 * i + a + 2)], a, ta_ref)
            total = term if total is None else total + term

        @pl.when(i == 0)
        def _():
            pre_ref[...] = total[0:256]

        hid = leaky(total)
        for k in range(2):

            def put(slot, x):
                h_ref[2 * i + k, slot, 0:16, :] = jnp.zeros((16, 256), BF)
                h_ref[2 * i + k, slot, 16:144, :] = x

            store_hidden(put, hid[256 * k : 256 * k + 128], hid[256 * k + 128 : 256 * k + 256])

    for i in range(steps):
        flush(i).wait()


def core_of():
    return lax.axis_index("dp") % 2


def plane_kernel(vol_ref, out_ref, sem):
    copy = pltpu.make_async_copy(vol_ref.at[0, vol_ref.shape[1] - 1], out_ref, sem)
    copy.start()
    copy.wait()


def pack_kernel(n, cot_ref, kb_ref, after_ref, *refs):
    del after_ref
    outs, full_ref = refs[:n], refs[n]
    chan = cot_ref.shape[4]
    lanes = 128 // chan
    rows = 256 // lanes
    per = 16 // n
    row = iota((256, 256), 0)
    col = iota((256, 256), 1)
    source = (row % 16) * 16 + ((row % rows) // 16) * lanes + row // rows
    pick = (col == source).astype(F32).astype(BF)
    for p in range(16):
        y = dot(pick, cot_ref[0, p].reshape(256, chan))
        z = jnp.concatenate([y[rows * l : rows * l + rows] for l in range(lanes)], axis=1).astype(BF)
        t = p // per
        at = (p % per) * rows
        full_ref[t, at : at + rows, :] = z
        if p % per == 0 and t > 0:
            full_ref[t - 1, per * rows : per * rows + rows, :] = z
    full_ref[n - 1, per * rows : per * rows + rows, :] = jnp.zeros((rows, 128), BF)
    me = lax.axis_index("mp")
    first = 13 * core_of()
    size = kb_ref.shape[1]
    head = (per + 1) * rows
    for d in range(n):
        outs[d][0:head, :] = full_ref[(me + d) % n]
        for j in range(HALF):
            outs[d][head + size * j : head + size * j + size, :] = kb_ref[first + j]


def gather_kernel(n, *refs):
    pieces, (cot_ref, kb_ref) = refs[:n], refs[n:]
    head, tail = cot_ref.shape[1], kb_ref.shape[1]
    me = lax.axis_index("mp")
    for d in range(n):
        cot_ref[(me + n - d) % n] = pieces[d][0:head, :]
        kb_ref[(me + n - d) % n] = pieces[d][head : head + tail, :]


def lane_order(n, inverse):
    size = n * 128
    chan = 128 // n
    row = iota((size, size), 0)
    col = iota((size, size), 1)
    if inverse:
        row, col = col, row
    target = ((row // chan) % n) * 128 + (row // 128) * chan + row % chan
    return (col == target).astype(F32).astype(BF)


def slab_planes(a, count):
    return [2 * p + a - 1 for p in range(count + 1)][1 if a == 0 else 0 :][:count]


def second_rows(hread, a, count):
    planes = slab_planes(a, count)
    parts = []
    for b in range(3):
        parts.append(jnp.concatenate([hread(u, b, 16, 0, 256) for u in planes], axis=0))
        parts.append(jnp.concatenate([hread(u, b, 0, 128, 128) for u in planes], axis=0))
    return jnp.concatenate(parts, axis=1)


def hidden_reader(h_ref, h0_ref):
    def read(index, slot, row, lane, width):
        rows, cols = slice(row, row + 128), slice(lane, lane + width)
        return h0_ref[slot, rows, cols] if index == 0 else h_ref[index, slot, rows, cols]

    return read


def put_in(ref):
    def put(slot, v):
        ref[slot, 0:16, :] = jnp.zeros((16, 256), BF)
        ref[slot, 16:144, :] = v

    return put


def put_half(both_ref, item, v):
    both_ref[(item + core_of()) % 2, item // 2] = v


def split_halves(count, both_ref, keep_ref, send_ref):
    zero = jnp.zeros(keep_ref.shape[1:], F32)
    for item in range(count, 2 * keep_ref.shape[0]):
        put_half(both_ref, item, zero)
    keep_ref[...] = both_ref[0]
    send_ref[...] = both_ref[1]


def halo_kernel(halo_ref, ka_ref, pre_ref, vd_out, h0_ref, vdh_ref, ta_ref, sem):
    build_first(ka_ref, ta_ref, 3)
    store_plane(vdh_ref, (), deinterleave(halo_ref[...], 1), 0)
    flush = pltpu.make_async_copy(vdh_ref, vd_out, sem)
    flush.start()
    hid = leaky(pre_ref[...] + first_term([sub(vdh_ref)], 0, ta_ref))
    store_hidden(put_in(h0_ref), hid[0:128], hid[128:256])
    flush.wait()


def grad_b_kernel(n, h_ref, h0_ref, cot_ref, c_ref, both_ref):
    slab = 16 // n
    lanes = n
    rows = 256 // lanes
    wide = jnp.concatenate([cot_ref[t] for t in range(n)], axis=1)
    turned = dot(wide, lane_order(n, False))
    turns = []
    for p in range(slab + 1):
        main = jnp.concatenate(
            [
                turned[
                    p * rows + 16 * (2 * s // lanes) : p * rows + 16 * (2 * s // lanes) + 16,
                    128 * (2 * s % lanes) : 128 * (2 * s % lanes) + 256,
                ]
                for s in range(8)
            ],
            axis=0,
        )
        turn = main.T
        one = jnp.concatenate([turn[0:128], turn[128:256]], axis=1)
        two = jnp.concatenate([turn[128:256], next_group(turn[0:128])], axis=1)
        turns.append(jnp.concatenate([one, two], axis=0).astype(BF))
        for slot, v in enumerate((main, up_shift(main))):
            c_ref[p, slot, 0:128, :] = v.astype(BF)
            c_ref[p, slot, 128:144, :] = jnp.zeros((16, 256), BF)
    read = hidden_reader(h_ref, h0_ref)
    for a in range(3):
        first = 1 if a == 0 else 0
        turn = jnp.concatenate(turns[first : first + slab], axis=1)
        columns = []
        for b in range(3):
            tiles = [read(u, b, 16, 128 * k, 128) for u in slab_planes(a, slab) for k in range(2)]
            columns.append(jnp.concatenate(tiles, axis=0))
        g = dot(turn, jnp.concatenate(columns, axis=1))
        for b in range(3):
            t = 3 * a + b
            one = g[0:128, 128 * b : 128 * b + 128].T
            two = g[128:256, 128 * b : 128 * b + 128].T
            both_ref[3 * t % 2, 3 * t // 2] = two[64:128]
            both_ref[(3 * t + 1) % 2, (3 * t + 1) // 2] = one[0:64]
            both_ref[(3 * t + 2) % 2, (3 * t + 2) // 2] = one[64:128]
    for item in range(TAPS, 2 * both_ref.shape[1]):
        both_ref[item % 2, item // 2] = jnp.zeros(both_ref.shape[2:], F32)


def second_taps(n, kb_ref, other_ref):
    chan = 64 // n
    first = core_of() == 0

    def tap(k):
        j, own_first = (k, True) if k < 13 else (k - 13, False)
        parts = []
        for z in range(n):
            own = kb_ref[z, j * chan : j * chan + chan, :]
            other = other_ref[z, j * chan : j * chan + chan, :]
            pair = (own, other) if own_first else (other, own)
            parts.append(jnp.where(first, *pair))
        return jnp.concatenate(parts, axis=0)

    return tap


def build_second(n, kb_ref, other_ref, tb_ref):
    tap = second_taps(n, kb_ref, other_ref)
    blank = jnp.zeros((64, 128), BF)
    for t in range(9):
        taps = [tap(3 * t + c) for c in range(3)]
        for w in range(-2, 4):
            row = 384 * t + (64 * w if w >= 0 else 256 + 64 * (w + 2))
            for r in range(2):
                c = w - 2 * r + 1
                tb_ref[row : row + 64, 128 * r : 128 * r + 128] = taps[c] if 0 <= c <= 2 else blank


REACH = (((4,), (3, 5)), ((1, 7), (0, 2, 6, 8)))


def build_transposed(n, kb_ref, other_ref, tb_ref):
    tap = second_taps(n, kb_ref, other_ref)
    blank = jnp.zeros((128, 128), BF)
    for at, t in enumerate(REACH[0][0] + REACH[0][1] + REACH[1][0] + REACH[1][1]):
        taps = [tap(3 * t + c).astype(F32) for c in range(3)]
        both = jnp.concatenate([taps[1], taps[2]], axis=0).T.astype(BF)
        low = jnp.concatenate([jnp.zeros((64, 128), F32), taps[0]], axis=0).T.astype(BF)
        for r, (left, right) in enumerate(((both, blank), (low, both), (blank, low))):
            row = 384 * at + 128 * r
            tb_ref[row : row + 128, 0:128] = left
            tb_ref[row : row + 128, 128:256] = right


def grad_a_kernel(n, kb_ref, other_ref, h_ref, h0_ref, c_ref, vd_ref, vdh_ref, keep_ref, send_ref, tb_ref, d_ref, both_ref):
    slab = 16 // n
    planes = 2 * slab
    build_transposed(n, kb_ref, other_ref, tb_ref)
    read = hidden_reader(h_ref, h0_ref)
    row = 0
    for par in range(2):
        for hp in range(2):
            parts = []
            for t in REACH[par][hp]:
                up = 1 if t < 3 else 0
                slot = 1 if t % 3 == 0 else 0
                parts.append(jnp.concatenate([c_ref[p + up, slot, 0:128, :] for p in range(slab)], axis=0))
                parts.append(jnp.concatenate([c_ref[p + up, slot, 16:144, 0:128] for p in range(slab)], axis=0))
            size = 192 * len(parts)
            back = dot(jnp.concatenate(parts, axis=1), tb_ref[row : row + size, :])
            row += size
            back = back.astype(BF).astype(F32)
            for p in range(slab):
                u = 2 * p + par
                mask = read(u, 1 + hp, 16, 0, 256).astype(F32) > 0
                v = back[128 * p : 128 * p + 128]
                v = jnp.where(mask, v, 0.3 * v).T
                at = 512 * u + 256 * hp
                d_ref[0:128, at : at + 128] = v[0:128].astype(BF)
                d_ref[128:192, at : at + 128] = v[128:192].astype(BF)
                d_ref[0:128, at + 128 : at + 256] = v[128:256].astype(BF)
                d_ref[128:192, at + 128 : at + 256] = next_group(v[0:64]).astype(BF)
    left = iota((64, 128), 1) < 32
    pieces = []
    for first in range(0, 9, 2):
        columns = []
        for t in range(first, min(first + 2, 9)):
            a, b = t // 3, t % 3
            tiles = []
            for u in range(planes):
                src = sub(vdh_ref) if 2 * u + a == 0 else sub(vd_ref, 2 * u + a - 1)
                tiles += [src(2 * hp + b, 16, 128 * k, 128) for hp in range(2) for k in range(2)]
            columns.append(jnp.concatenate(tiles, axis=0))
        both = dot(d_ref[...], jnp.concatenate(columns, axis=1))
        for j in range(len(columns)):
            g = both[:, 128 * j : 128 * j + 128]
            pieces.append(
                jnp.where(left, pltpu.roll(g[128:192], 32, 1), pltpu.roll(g[0:64], 32, 1))
                + pltpu.roll(g[64:128], 96, 1)
            )
    pieces.append(jnp.zeros((64, 128), F32))
    for k in range(PAIRS):
        both = jnp.concatenate([pieces[2 * k], pieces[2 * k + 1]], axis=0).T
        for j in range(6):
            put_half(both_ref, 6 * k + j, both[16 * j : 16 * j + 16])
    split_halves(6 * PAIRS, both_ref, keep_ref, send_ref)


def features_kernel(n, kb_ref, other_ref, h_ref, h0_ref, *refs):
    outs, (piece_ref, tb_ref) = refs[:n], refs[n:]
    slab = 16 // n
    lanes = n
    build_second(n, kb_ref, other_ref, tb_ref)
    read = hidden_reader(h_ref, h0_ref)
    terms = [dot(second_rows(read, a, slab), tb_ref[1152 * a : 1152 * a + 1152, :]) for a in range(3)]
    local = terms[1] + terms[2]
    total = jnp.concatenate(
        [local[0:128], local[128:] + terms[0][: 128 * slab - 128], terms[0][128 * slab - 128 :]], axis=0
    ).astype(BF)
    wide = []
    for p in range(slab + 1):
        for m in range(16 // lanes):
            at = 128 * p + 16 * (m * lanes // 2)
            wide.append(
                jnp.concatenate([total[at + 16 * k : at + 16 * k + 16] for k in range(lanes // 2)], axis=1)
            )
    packed = dot(jnp.concatenate(wide, axis=0), lane_order(n, True)).astype(BF)
    for z in range(n):
        piece_ref[z] = packed[:, 128 * z : 128 * z + 128]
    me = lax.axis_index("mp")
    for d in range(n):
        outs[d][...] = piece_ref[(me + d) % n]


def per_column(columns):
    return -(-14 // columns), -(-15 // columns)


def pair_kernel(columns, mine_b, got_b, keep_a, got_a, *outs):
    taps, chunks = per_column(columns)
    core = core_of()
    k = lax.axis_index("dp") // 2
    for m in range(columns):
        to = jnp.bitwise_xor(k, m)
        for s in range(taps):
            j = to * taps + s
            outs[m][64 * s : 64 * s + 64, :] = (mine_b[core, j] + got_b[core, j]).astype(BF)
        for s in range(chunks):
            j = to * chunks + s
            at = 64 * taps + 16 * s
            outs[m][at : at + 16, :] = (keep_a[j] + got_a[j]).astype(BF)


def column_sum_kernel(n, columns, *refs):
    ins, outs, piece_ref = refs[:columns], refs[columns : columns + n], refs[columns + n]
    taps, chunks = per_column(columns)
    chan = 64 // n
    total = ins[0][...].astype(F32)
    for m in range(1, columns):
        total = total + ins[m][...].astype(F32)
    total = total.astype(BF)
    for z in range(n):
        for s in range(taps):
            at = 64 * s + chan * z
            piece_ref[z, chan * s : chan * s + chan, :] = total[at : at + chan]
        piece_ref[z, chan * taps :, :] = total[64 * taps :]
    me = lax.axis_index("mp")
    for d in range(n):
        outs[d][...] = piece_ref[(me + d) % n]


def slab_sum_kernel(n, columns, scale_a, scale_b, *refs):
    ins, out_ref = refs[:n], refs[n]
    split = 64 // n * per_column(columns)[0]
    total = ins[0][...].astype(F32)
    for d in range(1, n):
        total = total + ins[d][...].astype(F32)
    out_ref[0:split, :] = (total[0:split] * scale_b).astype(BF)
    out_ref[split:, :] = (total[split:] * scale_a).astype(BF)


def unpack_kernel(n, *refs):
    ins, out_ref = refs[:n], refs[n]
    chan = out_ref.shape[4]
    lanes = 128 // chan
    rows = 256 // lanes
    per = 16 // n
    row = iota((256, 256), 0)
    col = iota((256, 256), 1)
    source = (col % 16) * 16 + ((col % rows) // 16) * lanes + col // rows
    pick = (row == source).astype(F32).astype(BF)
    me = lax.axis_index("mp")
    for d in range(n):
        first = (me + n - d) % n * per
        for p in range(per):
            z = ins[d][p * rows : p * rows + rows, :].astype(F32)
            if p == 0:
                more = ins[(d + 1) % n][per * rows : per * rows + rows, :].astype(F32)
                z = z + jnp.where(first > 0, more, 0.0)
            x = jnp.concatenate([z[:, chan * l : chan * l + chan] for l in range(lanes)], axis=0).astype(BF)
            out_ref[0, first + p] = dot(pick, x).astype(BF).reshape(16, 16, chan)


def last_kernel(columns, *refs):
    mine, other, (a_ref, b_ref, chunk_ref, tap_ref) = refs[:columns], refs[columns : 2 * columns], refs[2 * columns :]
    taps, chunks = per_column(columns)
    chan = b_ref.shape[1]
    core = core_of()
    k = lax.axis_index("dp") // 2
    for m in range(columns):
        owner = jnp.bitwise_xor(k, m)
        for piece, c in ((mine[m], core), (other[m], 1 - core)):
            for s in range(taps):
                tap_ref[2 * (owner * taps + s) + c] = piece[chan * s : chan * s + chan, :].astype(F32)
            for s in range(chunks):
                at = chan * taps + 16 * s
                chunk_ref[2 * (owner * chunks + s) + c] = piece[at : at + 16, :].astype(F32)
    b_ref[...] = tap_ref[0:TAPS]
    for j in range(15):
        v = jnp.concatenate([chunk_ref[2 * j], chunk_ref[2 * j + 1]], axis=0)
        for half in range(2):
            t = 2 * (j // 3) + half
            if t < 9:
                a_ref[t // 3, t % 3, j % 3] = v[:, 64 * half : 64 * half + 64]


def call(body, outs, ins, us, scratch=(), mib=16):
    return pl.pallas_call(
        body,
        out_shape=outs,
        grid=(1,),
        in_specs=[VMEM] * ins if isinstance(ins, int) else ins,
        out_specs=[VMEM] * len(outs) if isinstance(outs, (list, tuple)) else VMEM,
        scratch_shapes=list(scratch),
        compiler_params=params(mib),
        cost_estimate=cost(us),
    )


def shards(volume, kernel_a, kernel_b, cotangent):
    n = lax.axis_size("mp")
    dp = lax.axis_size("dp")
    planes = volume.shape[1]
    hplanes = planes // 2
    slab = hplanes // 2
    chan_b = kernel_b.shape[3]
    chan_o = cotangent.shape[4]
    rows = 256 // (128 // chan_o)
    shape = jax.ShapeDtypeStruct
    up = [(i, i + 1) for i in range(n - 1)]
    swap = [(i, i ^ 1) for i in range(dp)]
    columns = dp // 2
    taps, chunks = per_column(columns)

    def along_mp(x, d):
        return lax.ppermute(x, "mp", [(i, (i + d) % n) for i in range(n)])

    def along_dp(x, m):
        return lax.ppermute(x, "dp", [(i, i ^ (2 * m)) for i in range(dp)])

    volume, cotangent, kernel_b = (
        pltpu.with_memory_space_constraint(x, pltpu.HBM) for x in (volume, cotangent, kernel_b.reshape(TAPS, chan_b, 128))
    )
    sent = (slab + 1) * rows + HALF * chan_b
    halo = pl.pallas_call(
        plane_kernel,
        out_shape=pltpu.VMEM((64, 2048), BF),
        in_specs=[pl.BlockSpec(memory_space=pltpu.HBM)],
        out_specs=VMEM,
        scratch_shapes=[pltpu.SemaphoreType.DMA],
        compiler_params=params(2),
        cost_estimate=cost(1),
    )(volume)
    parts = list(
        pl.pallas_call(
            functools.partial(pack_kernel, n),
            grid=(1,),
            out_shape=[pltpu.VMEM((sent, 128), BF)] * n,
            in_specs=[
                pl.BlockSpec(cotangent.shape, lambda i: (0, 0, 0, 0, 0)),
                pl.BlockSpec((TAPS, chan_b, 128), lambda i: (0, 0, 0)),
                pl.BlockSpec(memory_space=pl.ANY),
            ],
            out_specs=[VMEM] * n,
            scratch_shapes=[pltpu.VMEM((n, (slab + 1) * rows, 128), BF)],
            compiler_params=params(8),
            cost_estimate=cost(2),
        )(cotangent, kernel_b, halo)
    )
    halo = lax.ppermute(halo, "mp", up)
    for d in range(1, n):
        parts[d] = lax.ppermute(parts[d], "mp", [(i, (i + d) % n) for i in range(n)])

    vd, hidden, pre = pl.pallas_call(
        first_kernel,
        out_shape=(
            pltpu.HBM((planes, 5, 144, 256), BF),
            pltpu.VMEM((hplanes, 3, 144, 256), BF),
            pltpu.VMEM((256, 256), F32),
        ),
        in_specs=[pl.BlockSpec(memory_space=pltpu.HBM), VMEM],
        out_specs=(pl.BlockSpec(memory_space=pltpu.HBM), VMEM, VMEM),
        scratch_shapes=[
            pltpu.VMEM((planes // 4, 4, 64, 2048), BF),
            pltpu.VMEM((planes + 1, 5, 144, 256), BF),
            pltpu.VMEM((3456, 256), BF),
            pltpu.SemaphoreType.DMA((planes // 4,)),
            pltpu.SemaphoreType.DMA((planes // 4,)),
        ],
        compiler_params=params(24),
        cost_estimate=cost(100),
    )(volume, kernel_a)
    hbm = pl.BlockSpec(memory_space=pltpu.HBM)
    vdh, h0 = pl.pallas_call(
        halo_kernel,
        out_shape=(pltpu.HBM((5, 144, 256), BF), pltpu.VMEM((3, 144, 256), BF)),
        in_specs=[VMEM, VMEM, VMEM],
        out_specs=(hbm, VMEM),
        scratch_shapes=[
            pltpu.VMEM((5, 144, 256), BF),
            pltpu.VMEM((1152, 256), BF),
            pltpu.SemaphoreType.DMA,
        ],
        compiler_params=params(16),
        cost_estimate=cost(10),
    )(halo, kernel_a, pre)
    h0, *parts = lax.optimization_barrier((h0, *parts))
    cot, kb = call(
        functools.partial(gather_kernel, n),
        (pltpu.VMEM((n, (slab + 1) * rows, 128), BF), pltpu.VMEM((n, HALF * chan_b, 128), BF)),
        n,
        1,
    )(*parts)
    kb_other = lax.ppermute(kb, "dp", swap)

    c, mine_b = call(
        functools.partial(grad_b_kernel, n),
        (pltpu.VMEM((slab + 1, 2, 144, 256), BF), pltpu.VMEM((2, columns * taps, 64, 128), F32)),
        3,
        3,
    )(hidden, h0, cot)
    got_b = lax.ppermute(mine_b, "dp", swap)

    keep_a, send_a = call(
        functools.partial(grad_a_kernel, n),
        (pltpu.VMEM((columns * chunks, 16, 128), F32), pltpu.VMEM((columns * chunks, 16, 128), F32)),
        7,
        8,
        [pltpu.VMEM((3456, 256), BF), pltpu.VMEM((192, hplanes * 512), BF), pltpu.VMEM((2, columns * chunks, 16, 128), F32)],
        24,
    )(kb, kb_other, hidden, h0, c, vd, vdh)
    got_a = lax.ppermute(send_a, "dp", swap)

    size = 64 * taps + 16 * chunks
    sums = list(
        call(functools.partial(pair_kernel, columns), [pltpu.VMEM((size, 128), BF)] * columns, 4, 1)(
            mine_b, got_b, keep_a, got_a
        )
    )
    for m in range(1, columns):
        sums[m] = along_dp(sums[m], m)
    pieces = list(
        call(
            functools.partial(features_kernel, n),
            [pltpu.VMEM(((slab + 1) * rows, 128), BF)] * n,
            4,
            4,
            [
                pltpu.VMEM((n, (slab + 1) * rows, 128), BF),
                pltpu.VMEM((3456, 256), BF),
            ],
        )(kb, kb_other, hidden, h0)
    )
    late = n // 2
    for d in range(1, n):
        if d != late:
            pieces[d] = along_mp(pieces[d], d)

    size = chan_b * taps + 16 * chunks
    sums = list(
        call(
            functools.partial(column_sum_kernel, n, columns),
            [pltpu.VMEM((size, 128), BF)] * n,
            columns,
            1,
            [pltpu.VMEM((n, size, 128), BF)],
        )(*sums)
    )
    *sums, last_piece = lax.optimization_barrier((*sums, pieces[late]))
    for d in range(1, n):
        sums[d] = along_mp(sums[d], d)
    both = lax.optimization_barrier((*sums, *pieces[:late], *pieces[late + 1 :]))
    sums, pieces = both[:n], list(both[n:])
    pieces.insert(late, along_mp(last_piece, late))

    samples = volume.shape[0] * dp
    scale_a = 1 / math.sqrt(samples * (GRID // 2) ** 3)
    scale_b = 1 / math.sqrt(samples * (GRID // 4) ** 3)
    total = call(
        functools.partial(slab_sum_kernel, n, columns, scale_a, scale_b), pltpu.VMEM((size, 128), BF), n, 1
    )(*sums)
    mine = [total] + [along_dp(total, m) for m in range(1, columns)]
    features = call(functools.partial(unpack_kernel, n), shape((1, 16, 16, 16, chan_o), BF), n, 2)(*pieces)
    both = lax.optimization_barrier((features, *mine))
    features, mine = both[0], both[1:]
    other = [lax.ppermute(x, "dp", swap) for x in mine]
    grad_a, grad_b = call(
        functools.partial(last_kernel, columns),
        (shape((3, 3, 3, 32, 64), F32), shape((TAPS, chan_b, 128), F32)),
        2 * columns,
        1,
        [
            pltpu.VMEM((2 * columns * chunks, 16, 128), F32),
            pltpu.VMEM((2 * columns * taps, chan_b, 128), F32),
        ],
    )(*mine, *other)
    return (features, grad_a, grad_b.reshape(3, 3, 3, chan_b, 128))


def solution(mesh):
    return jax.shard_map(
        shards,
        mesh=mesh,
        in_specs=(
            P("dp", "mp", None, None),
            P(),
            P(None, None, None, "mp", None),
            P("dp", None, None, None, "mp"),
        ),
        out_specs=(P("dp", None, None, None, "mp"), P(), P(None, None, None, "mp", None)),
        check_vma=False,
    )
```

```python
import functools
import math

import jax
import jax.numpy as jnp
from jax import lax
from jax.experimental import pallas as pl
from jax.experimental.pallas import tpu as pltpu
from jax.sharding import PartitionSpec as P

GRID = 64
BF = jnp.bfloat16
F32 = jnp.float32
VMEM = pl.BlockSpec(memory_space=pltpu.VMEM)
TAPS = 27
HALF = 14
PAIRS = 5
MIB = 1 << 20


def dot(a, b):
    return lax.dot_general(a, b, (((1,), (0,)), ((), ())), preferred_element_type=F32)


def iota(shape, dim):
    return lax.broadcasted_iota(jnp.int32, shape, dim)


def params(mib):
    return pltpu.CompilerParams(vmem_limit_bytes=mib * MIB)


def cost(us):
    return pl.CostEstimate(flops=int(us * 1e9), bytes_accessed=int(us * 3e6), transcendentals=0)


def deinterleave(x, count):
    row = iota((80 * count, 64 * count), 0)
    col = iota((80 * count, 64 * count), 1)
    h = 4 * (row % 16) + row % 80 // 16 - 1
    pick = jnp.logical_and(h >= 0, col == row // 80 * 64 + h).astype(F32).astype(BF)
    return dot(pick, x).astype(BF)


def store_plane(ref, lead, y, row):
    for slot in range(5):
        ref[(*lead, slot, slice(0, 16))] = jnp.zeros((16, 256), BF)
        for s in range(8):
            at = row + 16 * slot
            ref[(*lead, slot, slice(16 + 16 * s, 32 + 16 * s))] = y[at : at + 16, 256 * s : 256 * s + 256]


def build_first(ka_ref, ta_ref, taps=9):
    left = iota((32, 128), 1) < 64
    zero = jnp.zeros((32, 128), F32)
    for t in range(taps):
        wide = []
        for c in range(3):
            k = ka_ref[t // 3, t % 3, c].astype(F32)
            wide.append(jnp.concatenate([k, k], axis=1))
        for half in range(2):
            for w in range(-4, 8):
                row = 384 * t + (32 * w if w >= 0 else 256 + 32 * (w + 4))
                c0 = w - 4 * half + 1
                c1 = c0 - 2
                l = wide[c0] if 0 <= c0 <= 2 else zero
                r = wide[c1] if 0 <= c1 <= 2 else zero
                ta_ref[row : row + 32, 128 * half : 128 * half + 128] = jnp.where(left, l, r).astype(BF)


def first_rows(plane, b):
    main = jnp.concatenate([plane(b, 16, 0, 256), plane(b + 2, 16, 0, 256)], axis=0)
    edge = jnp.concatenate([plane(b, 0, 128, 128), plane(b + 2, 0, 128, 128)], axis=0)
    return [main, edge]


def first_term(planes, a, ta_ref):
    parts = []
    for b in range(3):
        both = [first_rows(plane, b) for plane in planes]
        parts.append(jnp.concatenate([m for m, _ in both], axis=0))
        parts.append(jnp.concatenate([e for _, e in both], axis=0))
    return dot(jnp.concatenate(parts, axis=1), ta_ref[1152 * a : 1152 * a + 1152, :])


def down_shift(x):
    moved = pltpu.roll(x, 1, 0)
    return jnp.where(iota(x.shape, 0) % 16 == 0, 0.0, moved)


def next_group(x):
    moved = pltpu.roll(x, 112, 1)
    return jnp.where(iota(x.shape, 1) >= 112, 0.0, moved)


def up_shift(x):
    moved = pltpu.roll(x, x.shape[0] - 1, 0)
    return jnp.where(iota(x.shape, 0) % 16 == 15, 0.0, moved)


def store_hidden(put, even, odd):
    put(0, down_shift(odd).astype(BF))
    put(1, even.astype(BF))
    put(2, odd.astype(BF))


def leaky(pre):
    return jnp.where(pre > 0, pre, 0.3 * pre)


def sub(ref, *lead):
    def read(slot, row, lane, width):
        return ref[(*lead, slot, slice(row, row + 128), slice(lane, lane + width))]

    return read


def first_kernel(vol_ref, ka_ref, out_ref, h_ref, pre_ref, x_ref, vd_ref, ta_ref, sems, out_sems):
    steps = x_ref.shape[0]

    def fetch(i):
        return pltpu.make_async_copy(vol_ref.at[0, pl.ds(4 * i, 4)], x_ref.at[i], sems.at[i])

    def flush(i):
        return pltpu.make_async_copy(
            vd_ref.at[pl.ds(4 * i + 1, 4)], out_ref.at[pl.ds(4 * i, 4)], out_sems.at[i]
        )

    for i in range(steps):
        fetch(i).start()
    build_first(ka_ref, ta_ref)
    vd_ref[0] = jnp.zeros((5, 144, 256), BF)

    @pl.loop(0, steps)
    def _(i):
        fetch(i).wait()
        y = deinterleave(x_ref[i].reshape(256, 2048), 4)
        for k in range(4):
            store_plane(vd_ref, (4 * i + k + 1,), y, 80 * k)
        flush(i).start()
        total = None
        for a in range(3):
            term = first_term([sub(vd_ref, 4 * i + a), sub(vd_ref, 4 * i + a + 2)], a, ta_ref)
            total = term if total is None else total + term

        @pl.when(i == 0)
        def _():
            pre_ref[...] = total[0:256]

        hid = leaky(total)
        for k in range(2):

            def put(slot, x):
                h_ref[2 * i + k, slot, 0:16, :] = jnp.zeros((16, 256), BF)
                h_ref[2 * i + k, slot, 16:144, :] = x

            store_hidden(put, hid[256 * k : 256 * k + 128], hid[256 * k + 128 : 256 * k + 256])

    for i in range(steps):
        flush(i).wait()


def core_of():
    return lax.axis_index("dp") % 2


def plane_kernel(vol_ref, out_ref, sem):
    copy = pltpu.make_async_copy(vol_ref.at[0, vol_ref.shape[1] - 1], out_ref, sem)
    copy.start()
    copy.wait()


def pack_kernel(n, cot_ref, kb_ref, after_ref, *refs):
    del after_ref
    outs, full_ref = refs[:n], refs[n]
    chan = cot_ref.shape[4]
    lanes = 128 // chan
    rows = 256 // lanes
    per = 16 // n
    row = iota((256, 256), 0)
    col = iota((256, 256), 1)
    source = (row % 16) * 16 + ((row % rows) // 16) * lanes + row // rows
    pick = (col == source).astype(F32).astype(BF)
    for p in range(16):
        y = dot(pick, cot_ref[0, p].reshape(256, chan))
        z = jnp.concatenate([y[rows * l : rows * l + rows] for l in range(lanes)], axis=1).astype(BF)
        t = p // per
        at = (p % per) * rows
        full_ref[t, at : at + rows, :] = z
        if p % per == 0 and t > 0:
            full_ref[t - 1, per * rows : per * rows + rows, :] = z
    full_ref[n - 1, per * rows : per * rows + rows, :] = jnp.zeros((rows, 128), BF)
    me = lax.axis_index("mp")
    first = 13 * core_of()
    size = kb_ref.shape[1]
    head = (per + 1) * rows
    for d in range(n):
        outs[d][0:head, :] = full_ref[(me + d) % n]
        for j in range(HALF):
            outs[d][head + size * j : head + size * j + size, :] = kb_ref[first + j]


def gather_kernel(n, *refs):
    pieces, (cot_ref, kb_ref) = refs[:n], refs[n:]
    head, tail = cot_ref.shape[1], kb_ref.shape[1]
    me = lax.axis_index("mp")
    for d in range(n):
        cot_ref[(me + n - d) % n] = pieces[d][0:head, :]
        kb_ref[(me + n - d) % n] = pieces[d][head : head + tail, :]


def lane_order(n, inverse):
    size = n * 128
    chan = 128 // n
    row = iota((size, size), 0)
    col = iota((size, size), 1)
    if inverse:
        row, col = col, row
    target = ((row // chan) % n) * 128 + (row // 128) * chan + row % chan
    return (col == target).astype(F32).astype(BF)


def slab_planes(a, count):
    return [2 * p + a - 1 for p in range(count + 1)][1 if a == 0 else 0 :][:count]


def second_rows(hread, a, count):
    planes = slab_planes(a, count)
    parts = []
    for b in range(3):
        parts.append(jnp.concatenate([hread(u, b, 16, 0, 256) for u in planes], axis=0))
        parts.append(jnp.concatenate([hread(u, b, 0, 128, 128) for u in planes], axis=0))
    return jnp.concatenate(parts, axis=1)


def hidden_reader(h_ref, h0_ref):
    def read(index, slot, row, lane, width):
        rows, cols = slice(row, row + 128), slice(lane, lane + width)
        return h0_ref[slot, rows, cols] if index == 0 else h_ref[index, slot, rows, cols]

    return read


def put_in(ref):
    def put(slot, v):
        ref[slot, 0:16, :] = jnp.zeros((16, 256), BF)
        ref[slot, 16:144, :] = v

    return put


def put_half(both_ref, item, v):
    both_ref[(item + core_of()) % 2, item // 2] = v


def split_halves(count, both_ref, keep_ref, send_ref):
    zero = jnp.zeros(keep_ref.shape[1:], F32)
    for item in range(count, 2 * keep_ref.shape[0]):
        put_half(both_ref, item, zero)
    keep_ref[...] = both_ref[0]
    send_ref[...] = both_ref[1]


def halo_kernel(halo_ref, ka_ref, pre_ref, vd_out, h0_ref, vdh_ref, ta_ref, sem):
    build_first(ka_ref, ta_ref, 3)
    store_plane(vdh_ref, (), deinterleave(halo_ref[...], 1), 0)
    flush = pltpu.make_async_copy(vdh_ref, vd_out, sem)
    flush.start()
    hid = leaky(pre_ref[...] + first_term([sub(vdh_ref)], 0, ta_ref))
    store_hidden(put_in(h0_ref), hid[0:128], hid[128:256])
    flush.wait()


def grad_b_kernel(n, h_ref, h0_ref, cot_ref, c_ref, both_ref):
    slab = 16 // n
    lanes = n
    rows = 256 // lanes
    wide = jnp.concatenate([cot_ref[t] for t in range(n)], axis=1)
    turned = dot(wide, lane_order(n, False))
    turns = []
    for p in range(slab + 1):
        main = jnp.concatenate(
            [
                turned[
                    p * rows + 16 * (2 * s // lanes) : p * rows + 16 * (2 * s // lanes) + 16,
                    128 * (2 * s % lanes) : 128 * (2 * s % lanes) + 256,
                ]
                for s in range(8)
            ],
            axis=0,
        )
        turn = main.T
        one = jnp.concatenate([turn[0:128], turn[128:256]], axis=1)
        two = jnp.concatenate([turn[128:256], next_group(turn[0:128])], axis=1)
        turns.append(jnp.concatenate([one, two], axis=0).astype(BF))
        for slot, v in enumerate((main, up_shift(main))):
            c_ref[p, slot, 0:128, :] = v.astype(BF)
            c_ref[p, slot, 128:144, :] = jnp.zeros((16, 256), BF)
    read = hidden_reader(h_ref, h0_ref)
    for a in range(3):
        first = 1 if a == 0 else 0
        turn = jnp.concatenate(turns[first : first + slab], axis=1)
        columns = []
        for b in range(3):
            tiles = [read(u, b, 16, 128 * k, 128) for u in slab_planes(a, slab) for k in range(2)]
            columns.append(jnp.concatenate(tiles, axis=0))
        g = dot(turn, jnp.concatenate(columns, axis=1))
        for b in range(3):
            t = 3 * a + b
            one = g[0:128, 128 * b : 128 * b + 128].T
            two = g[128:256, 128 * b : 128 * b + 128].T
            both_ref[3 * t % 2, 3 * t // 2] = two[64:128]
            both_ref[(3 * t + 1) % 2, (3 * t + 1) // 2] = one[0:64]
            both_ref[(3 * t + 2) % 2, (3 * t + 2) // 2] = one[64:128]
    for item in range(TAPS, 2 * both_ref.shape[1]):
        both_ref[item % 2, item // 2] = jnp.zeros(both_ref.shape[2:], F32)


def second_taps(n, kb_ref, other_ref):
    chan = 64 // n
    first = core_of() == 0

    def tap(k):
        j, own_first = (k, True) if k < 13 else (k - 13, False)
        parts = []
        for z in range(n):
            own = kb_ref[z, j * chan : j * chan + chan, :]
            other = other_ref[z, j * chan : j * chan + chan, :]
            pair = (own, other) if own_first else (other, own)
            parts.append(jnp.where(first, *pair))
        return jnp.concatenate(parts, axis=0)

    return tap


def build_second(n, kb_ref, other_ref, tb_ref):
    tap = second_taps(n, kb_ref, other_ref)
    blank = jnp.zeros((64, 128), BF)
    for t in range(9):
        taps = [tap(3 * t + c) for c in range(3)]
        for w in range(-2, 4):
            row = 384 * t + (64 * w if w >= 0 else 256 + 64 * (w + 2))
            for r in range(2):
                c = w - 2 * r + 1
                tb_ref[row : row + 64, 128 * r : 128 * r + 128] = taps[c] if 0 <= c <= 2 else blank


REACH = (((4,), (3, 5)), ((1, 7), (0, 2, 6, 8)))


def build_transposed(n, kb_ref, other_ref, tb_ref):
    tap = second_taps(n, kb_ref, other_ref)
    blank = jnp.zeros((128, 128), BF)
    for at, t in enumerate(REACH[0][0] + REACH[0][1] + REACH[1][0] + REACH[1][1]):
        taps = [tap(3 * t + c).astype(F32) for c in range(3)]
        both = jnp.concatenate([taps[1], taps[2]], axis=0).T.astype(BF)
        low = jnp.concatenate([jnp.zeros((64, 128), F32), taps[0]], axis=0).T.astype(BF)
        for r, (left, right) in enumerate(((both, blank), (low, both), (blank, low))):
            row = 384 * at + 128 * r
            tb_ref[row : row + 128, 0:128] = left
            tb_ref[row : row + 128, 128:256] = right


def grad_a_kernel(n, kb_ref, other_ref, h_ref, h0_ref, c_ref, vd_ref, vdh_ref, keep_ref, send_ref, tb_ref, d_ref, both_ref):
    slab = 16 // n
    planes = 2 * slab
    build_transposed(n, kb_ref, other_ref, tb_ref)
    read = hidden_reader(h_ref, h0_ref)
    row = 0
    for par in range(2):
        for hp in range(2):
            parts = []
            for t in REACH[par][hp]:
                up = 1 if t < 3 else 0
                slot = 1 if t % 3 == 0 else 0
                parts.append(jnp.concatenate([c_ref[p + up, slot, 0:128, :] for p in range(slab)], axis=0))
                parts.append(jnp.concatenate([c_ref[p + up, slot, 16:144, 0:128] for p in range(slab)], axis=0))
            size = 192 * len(parts)
            back = dot(jnp.concatenate(parts, axis=1), tb_ref[row : row + size, :])
            row += size
            back = back.astype(BF).astype(F32)
            for p in range(slab):
                u = 2 * p + par
                mask = read(u, 1 + hp, 16, 0, 256).astype(F32) > 0
                v = back[128 * p : 128 * p + 128]
                v = jnp.where(mask, v, 0.3 * v).T
                at = 512 * u + 256 * hp
                d_ref[0:128, at : at + 128] = v[0:128].astype(BF)
                d_ref[128:192, at : at + 128] = v[128:192].astype(BF)
                d_ref[0:128, at + 128 : at + 256] = v[128:256].astype(BF)
                d_ref[128:192, at + 128 : at + 256] = next_group(v[0:64]).astype(BF)
    left = iota((64, 128), 1) < 32
    pieces = []
    for first in range(0, 9, 2):
        columns = []
        for t in range(first, min(first + 2, 9)):
            a, b = t // 3, t % 3
            tiles = []
            for u in range(planes):
                src = sub(vdh_ref) if 2 * u + a == 0 else sub(vd_ref, 2 * u + a - 1)
                tiles += [src(2 * hp + b, 16, 128 * k, 128) for hp in range(2) for k in range(2)]
            columns.append(jnp.concatenate(tiles, axis=0))
        both = dot(d_ref[...], jnp.concatenate(columns, axis=1))
        for j in range(len(columns)):
            g = both[:, 128 * j : 128 * j + 128]
            pieces.append(
                jnp.where(left, pltpu.roll(g[128:192], 32, 1), pltpu.roll(g[0:64], 32, 1))
                + pltpu.roll(g[64:128], 96, 1)
            )
    pieces.append(jnp.zeros((64, 128), F32))
    for k in range(PAIRS):
        both = jnp.concatenate([pieces[2 * k], pieces[2 * k + 1]], axis=0).T
        for j in range(6):
            put_half(both_ref, 6 * k + j, both[16 * j : 16 * j + 16])
    split_halves(6 * PAIRS, both_ref, keep_ref, send_ref)


def features_kernel(n, kb_ref, other_ref, h_ref, h0_ref, *refs):
    outs, (piece_ref, tb_ref) = refs[:n], refs[n:]
    slab = 16 // n
    lanes = n
    build_second(n, kb_ref, other_ref, tb_ref)
    read = hidden_reader(h_ref, h0_ref)
    terms = [dot(second_rows(read, a, slab), tb_ref[1152 * a : 1152 * a + 1152, :]) for a in range(3)]
    local = terms[1] + terms[2]
    total = jnp.concatenate(
        [local[0:128], local[128:] + terms[0][: 128 * slab - 128], terms[0][128 * slab - 128 :]], axis=0
    ).astype(BF)
    wide = []
    for p in range(slab + 1):
        for m in range(16 // lanes):
            at = 128 * p + 16 * (m * lanes // 2)
            wide.append(
                jnp.concatenate([total[at + 16 * k : at + 16 * k + 16] for k in range(lanes // 2)], axis=1)
            )
    packed = dot(jnp.concatenate(wide, axis=0), lane_order(n, True)).astype(BF)
    for z in range(n):
        piece_ref[z] = packed[:, 128 * z : 128 * z + 128]
    me = lax.axis_index("mp")
    for d in range(n):
        outs[d][...] = piece_ref[(me + d) % n]


def per_column(columns):
    return -(-14 // columns), -(-15 // columns)


def pair_kernel(columns, mine_b, got_b, keep_a, got_a, *outs):
    taps, chunks = per_column(columns)
    core = core_of()
    k = lax.axis_index("dp") // 2
    for m in range(columns):
        to = jnp.bitwise_xor(k, m)
        for s in range(taps):
            j = to * taps + s
            outs[m][64 * s : 64 * s + 64, :] = (mine_b[core, j] + got_b[core, j]).astype(BF)
        for s in range(chunks):
            j = to * chunks + s
            at = 64 * taps + 16 * s
            outs[m][at : at + 16, :] = (keep_a[j] + got_a[j]).astype(BF)


def column_sum_kernel(n, columns, *refs):
    ins, outs, piece_ref = refs[:columns], refs[columns : columns + n], refs[columns + n]
    taps, chunks = per_column(columns)
    chan = 64 // n
    total = ins[0][...].astype(F32)
    for m in range(1, columns):
        total = total + ins[m][...].astype(F32)
    total = total.astype(BF)
    for z in range(n):
        for s in range(taps):
            at = 64 * s + chan * z
            piece_ref[z, chan * s : chan * s + chan, :] = total[at : at + chan]
        piece_ref[z, chan * taps :, :] = total[64 * taps :]
    me = lax.axis_index("mp")
    for d in range(n):
        outs[d][...] = piece_ref[(me + d) % n]


def slab_sum_kernel(n, columns, scale_a, scale_b, *refs):
    ins, out_ref = refs[:n], refs[n]
    split = 64 // n * per_column(columns)[0]
    total = ins[0][...].astype(F32)
    for d in range(1, n):
        total = total + ins[d][...].astype(F32)
    out_ref[0:split, :] = (total[0:split] * scale_b).astype(BF)
    out_ref[split:, :] = (total[split:] * scale_a).astype(BF)


def unpack_kernel(n, *refs):
    ins, out_ref = refs[:n], refs[n]
    chan = out_ref.shape[4]
    lanes = 128 // chan
    rows = 256 // lanes
    per = 16 // n
    row = iota((256, 256), 0)
    col = iota((256, 256), 1)
    source = (col % 16) * 16 + ((col % rows) // 16) * lanes + col // rows
    pick = (row == source).astype(F32).astype(BF)
    me = lax.axis_index("mp")
    for d in range(n):
        first = (me + n - d) % n * per
        for p in range(per):
            z = ins[d][p * rows : p * rows + rows, :].astype(F32)
            if p == 0:
                more = ins[(d + 1) % n][per * rows : per * rows + rows, :].astype(F32)
                z = z + jnp.where(first > 0, more, 0.0)
            x = jnp.concatenate([z[:, chan * l : chan * l + chan] for l in range(lanes)], axis=0).astype(BF)
            out_ref[0, first + p] = dot(pick, x).astype(BF).reshape(16, 16, chan)


def last_kernel(columns, *refs):
    mine, other, (a_ref, b_ref, chunk_ref, tap_ref) = refs[:columns], refs[columns : 2 * columns], refs[2 * columns :]
    taps, chunks = per_column(columns)
    chan = b_ref.shape[1]
    core = core_of()
    k = lax.axis_index("dp") // 2
    for m in range(columns):
        owner = jnp.bitwise_xor(k, m)
        for piece, c in ((mine[m], core), (other[m], 1 - core)):
            for s in range(taps):
                tap_ref[2 * (owner * taps + s) + c] = piece[chan * s : chan * s + chan, :].astype(F32)
            for s in range(chunks):
                at = chan * taps + 16 * s
                chunk_ref[2 * (owner * chunks + s) + c] = piece[at : at + 16, :].astype(F32)
    b_ref[...] = tap_ref[0:TAPS]
    for j in range(15):
        v = jnp.concatenate([chunk_ref[2 * j], chunk_ref[2 * j + 1]], axis=0)
        for half in range(2):
            t = 2 * (j // 3) + half
            if t < 9:
                a_ref[t // 3, t % 3, j % 3] = v[:, 64 * half : 64 * half + 64]


def call(body, outs, ins, us, scratch=(), mib=16):
    return pl.pallas_call(
        body,
        out_shape=outs,
        grid=(1,),
        in_specs=[VMEM] * ins if isinstance(ins, int) else ins,
        out_specs=[VMEM] * len(outs) if isinstance(outs, (list, tuple)) else VMEM,
        scratch_shapes=list(scratch),
        compiler_params=params(mib),
        cost_estimate=cost(us),
    )


def shards(volume, kernel_a, kernel_b, cotangent):
    n = lax.axis_size("mp")
    dp = lax.axis_size("dp")
    planes = volume.shape[1]
    hplanes = planes // 2
    slab = hplanes // 2
    chan_b = kernel_b.shape[3]
    chan_o = cotangent.shape[4]
    rows = 256 // (128 // chan_o)
    shape = jax.ShapeDtypeStruct
    up = [(i, i + 1) for i in range(n - 1)]
    swap = [(i, i ^ 1) for i in range(dp)]
    columns = dp // 2
    taps, chunks = per_column(columns)

    def along_mp(x, d):
        return lax.ppermute(x, "mp", [(i, (i + d) % n) for i in range(n)])

    def along_dp(x, m):
        return lax.ppermute(x, "dp", [(i, i ^ (2 * m)) for i in range(dp)])

    volume, cotangent, kernel_b = (
        pltpu.with_memory_space_constraint(x, pltpu.HBM) for x in (volume, cotangent, kernel_b.reshape(TAPS, chan_b, 128))
    )
    sent = (slab + 1) * rows + HALF * chan_b
    halo = pl.pallas_call(
        plane_kernel,
        out_shape=pltpu.VMEM((64, 2048), BF),
        in_specs=[pl.BlockSpec(memory_space=pltpu.HBM)],
        out_specs=VMEM,
        scratch_shapes=[pltpu.SemaphoreType.DMA],
        compiler_params=params(2),
        cost_estimate=cost(1),
    )(volume)
    parts = list(
        pl.pallas_call(
            functools.partial(pack_kernel, n),
            grid=(1,),
            out_shape=[pltpu.VMEM((sent, 128), BF)] * n,
            in_specs=[
                pl.BlockSpec(cotangent.shape, lambda i: (0, 0, 0, 0, 0)),
                pl.BlockSpec((TAPS, chan_b, 128), lambda i: (0, 0, 0)),
                pl.BlockSpec(memory_space=pl.ANY),
            ],
            out_specs=[VMEM] * n,
            scratch_shapes=[pltpu.VMEM((n, (slab + 1) * rows, 128), BF)],
            compiler_params=params(8),
            cost_estimate=cost(2),
        )(cotangent, kernel_b, halo)
    )
    halo = lax.ppermute(halo, "mp", up)
    for d in range(1, n):
        parts[d] = lax.ppermute(parts[d], "mp", [(i, (i + d) % n) for i in range(n)])

    vd, hidden, pre = pl.pallas_call(
        first_kernel,
        out_shape=(
            pltpu.HBM((planes, 5, 144, 256), BF),
            pltpu.VMEM((hplanes, 3, 144, 256), BF),
            pltpu.VMEM((256, 256), F32),
        ),
        in_specs=[pl.BlockSpec(memory_space=pltpu.HBM), VMEM],
        out_specs=(pl.BlockSpec(memory_space=pltpu.HBM), VMEM, VMEM),
        scratch_shapes=[
            pltpu.VMEM((planes // 4, 4, 64, 2048), BF),
            pltpu.VMEM((planes + 1, 5, 144, 256), BF),
            pltpu.VMEM((3456, 256), BF),
            pltpu.SemaphoreType.DMA((planes // 4,)),
            pltpu.SemaphoreType.DMA((planes // 4,)),
        ],
        compiler_params=params(24),
        cost_estimate=cost(100),
    )(volume, kernel_a)
    hbm = pl.BlockSpec(memory_space=pltpu.HBM)
    vdh, h0 = pl.pallas_call(
        halo_kernel,
        out_shape=(pltpu.HBM((5, 144, 256), BF), pltpu.VMEM((3, 144, 256), BF)),
        in_specs=[VMEM, VMEM, VMEM],
        out_specs=(hbm, VMEM),
        scratch_shapes=[
            pltpu.VMEM((5, 144, 256), BF),
            pltpu.VMEM((1152, 256), BF),
            pltpu.SemaphoreType.DMA,
        ],
        compiler_params=params(16),
        cost_estimate=cost(10),
    )(halo, kernel_a, pre)
    h0, *parts = lax.optimization_barrier((h0, *parts))
    cot, kb = call(
        functools.partial(gather_kernel, n),
        (pltpu.VMEM((n, (slab + 1) * rows, 128), BF), pltpu.VMEM((n, HALF * chan_b, 128), BF)),
        n,
        1,
    )(*parts)
    kb_other = lax.ppermute(kb, "dp", swap)

    c, mine_b = call(
        functools.partial(grad_b_kernel, n),
        (pltpu.VMEM((slab + 1, 2, 144, 256), BF), pltpu.VMEM((2, columns * taps, 64, 128), F32)),
        3,
        3,
    )(hidden, h0, cot)
    got_b = lax.ppermute(mine_b, "dp", swap)

    keep_a, send_a = call(
        functools.partial(grad_a_kernel, n),
        (pltpu.VMEM((columns * chunks, 16, 128), F32), pltpu.VMEM((columns * chunks, 16, 128), F32)),
        7,
        8,
        [pltpu.VMEM((3456, 256), BF), pltpu.VMEM((192, hplanes * 512), BF), pltpu.VMEM((2, columns * chunks, 16, 128), F32)],
        24,
    )(kb, kb_other, hidden, h0, c, vd, vdh)
    got_a = lax.ppermute(send_a, "dp", swap)

    size = 64 * taps + 16 * chunks
    sums = list(
        call(functools.partial(pair_kernel, columns), [pltpu.VMEM((size, 128), BF)] * columns, 4, 1)(
            mine_b, got_b, keep_a, got_a
        )
    )
    for m in range(1, columns):
        sums[m] = along_dp(sums[m], m)
    pieces = list(
        call(
            functools.partial(features_kernel, n),
            [pltpu.VMEM(((slab + 1) * rows, 128), BF)] * n,
            4,
            4,
            [
                pltpu.VMEM((n, (slab + 1) * rows, 128), BF),
                pltpu.VMEM((3456, 256), BF),
            ],
        )(kb, kb_other, hidden, h0)
    )
    pieces[1] = along_mp(pieces[1], 1)

    size = chan_b * taps + 16 * chunks
    sums = list(
        call(
            functools.partial(column_sum_kernel, n, columns),
            [pltpu.VMEM((size, 128), BF)] * n,
            columns,
            1,
            [pltpu.VMEM((n, size, 128), BF)],
        )(*sums)
    )
    both = lax.optimization_barrier((*sums, *pieces[2:]))
    sums, later = list(both[:n]), both[n:]
    for d in range(1, n):
        sums[d] = along_mp(sums[d], d)
    *sums, own, after = lax.optimization_barrier((*sums, *pieces[:2]))
    pieces = [own, after] + [along_mp(x, d) for d, x in enumerate(later, 2)]

    samples = volume.shape[0] * dp
    scale_a = 1 / math.sqrt(samples * (GRID // 2) ** 3)
    scale_b = 1 / math.sqrt(samples * (GRID // 4) ** 3)
    total = call(
        functools.partial(slab_sum_kernel, n, columns, scale_a, scale_b), pltpu.VMEM((size, 128), BF), n, 1
    )(*sums)
    mine = [total] + [along_dp(total, m) for m in range(1, columns)]
    features = call(functools.partial(unpack_kernel, n), shape((1, 16, 16, 16, chan_o), BF), n, 2)(*pieces)
    both = lax.optimization_barrier((features, *mine))
    features, mine = both[0], both[1:]
    other = [lax.ppermute(x, "dp", swap) for x in mine]
    grad_a, grad_b = call(
        functools.partial(last_kernel, columns),
        (shape((3, 3, 3, 32, 64), F32), shape((TAPS, chan_b, 128), F32)),
        2 * columns,
        1,
        [
            pltpu.VMEM((2 * columns * chunks, 16, 128), F32),
            pltpu.VMEM((2 * columns * taps, chan_b, 128), F32),
        ],
    )(*mine, *other)
    return (features, grad_a, grad_b.reshape(3, 3, 3, chan_b, 128))


def solution(mesh):
    return jax.shard_map(
        shards,
        mesh=mesh,
        in_specs=(
            P("dp", "mp", None, None),
            P(),
            P(None, None, None, "mp", None),
            P("dp", None, None, None, "mp"),
        ),
        out_specs=(P("dp", None, None, None, "mp"), P(), P(None, None, None, "mp", None)),
        check_vma=False,
    )
```
